32 devices in a mesh: row: 4 (over x, core), col: 8 (over z, y).
Axes of the slice: x: 2, y: 2, z: 4, core: 2. Of those that a mesh axis runs over, the one named last changes fastest.
Arguments:
- tokens: bfloat16 [512, 6144], P('row', 'col'), may hold values from -6 to 6
- weight_in: bfloat16 [6144, 24576], P('row', 'col'), may hold values from -0.109375 to 0.109375
- weight_out: bfloat16 [24576, 6144], P('col', 'row'), may hold values from -0.0546875 to 0.0546875
- out_grad: bfloat16 [512, 6144], P('row', 'col'), may hold values from -1.5 to 1.5
Outputs:
- block_out: bfloat16 [512, 6144], P('row', 'col')
- grad_tokens: bfloat16 [512, 6144], P('row', 'col')
- grad_in: bfloat16 [6144, 24576], P('row', 'col')
- grad_out: bfloat16 [24576, 6144], P('col', 'row')
The draws below stay inside these ranges and needn't reach their ends.
All inputs are finite; a program needn't handle non-finite values.
Results may differ from the reference program's by a relative error of at most 0.0051.
Values may be sent and summed in bfloat16 or wider, within the bound.
No kernel may reach another device: no remote copies, remote signals or barrier semaphores. Data moves between devices by JAX's collectives and lax.ppermute only.
A program may use at most 256 MiB of HBM per device.

```python
import jax
import jax.numpy as jnp
from jax import lax

D = 6144
FF = 24576
TOKENS = 512


def spiked(drawn, own_key, source, target, blocks, factor):
    def block_of(dim):
        return (jnp.arange(drawn.shape[dim]) // (drawn.shape[dim] // blocks)).reshape((-1,) + (1,) * (drawn.ndim - 1 - dim))

    first = jax.random.permutation(own_key, blocks)[block_of(target)]
    far = (block_of(target) + blocks // 2) % blocks
    return jnp.where((block_of(source) == first) | (block_of(source) == far), factor * drawn, drawn)


def steps_of(stream_key, shape, pieces, smallest, high):
    loudness = 1.0
    for dim, parts in pieces:
        draws = jax.random.uniform(jax.random.fold_in(jax.random.fold_in(stream_key, 6), dim), (parts,), jnp.float32, smallest / len(pieces), high / len(pieces))
        loudness = loudness * jnp.repeat(jnp.exp(draws), shape[dim] // parts).reshape((-1,) + (1,) * (len(shape) - 1 - dim))
    return loudness


def bell_draw(stream_key, dims, spread, reach, shards=(), dtype=jnp.bfloat16):
    factor_of = steps_of(stream_key, dims, shards, -0.22, 0.18) if shards else 1.0
    values = jax.random.normal(stream_key, dims, jnp.float32) * spread * factor_of
    return jnp.minimum(jnp.maximum(values, -reach), reach).astype(dtype)


def gaussian_with(key, dims, spread, bound, shards, heavy, kind=jnp.bfloat16):
    entries = spread * jax.random.normal(key, dims, jnp.float32)
    if shards:
        entries = entries * steps_of(key, dims, shards, -0.22, 0.18)
    return jnp.clip(spiked(entries, jax.random.fold_in(key, 3), *heavy), -bound, bound).astype(kind)


def setup_inputs(seed: int = 0) -> dict:
    splits = jax.random.split(jax.random.key(seed), 5)
    tokens = bell_draw(splits[0], (TOKENS, D), 1.0, 6.0, ((0, 4), (1, 8)))
    weight_in = gaussian_with(splits[1], (D, FF), D ** -0.5, 0.109375, ((0, 4), (1, 8)), (1, 0, 8, 2.0))
    weight_out = gaussian_with(splits[2], (FF, D), FF ** -0.5, 0.0546875, ((0, 8), (1, 4)), (0, 1, 8, 2.0))
    out_grad = bell_draw(splits[3], (TOKENS, D), 0.25, 1.5, ((0, 4), (1, 8)))
    return {"tokens": tokens, "weight_in": weight_in, "weight_out": weight_out, "out_grad": out_grad}


def cdf_of(value):
    return 0.5 * (1.0 + lax.erf(value * 0.7071067811865476))


def reference(tokens, weight_in, weight_out, out_grad):
    hidden_pre = jnp.dot(tokens, weight_in, preferred_element_type=jnp.float32)
    cumul = cdf_of(hidden_pre)
    act = (hidden_pre * cumul).astype(jnp.bfloat16)
    block_out = jnp.dot(act, weight_out, preferred_element_type=jnp.float32).astype(jnp.bfloat16)
    grad_act = jnp.dot(out_grad, weight_out.T, preferred_element_type=jnp.float32)
    density = jnp.exp(-0.5 * hidden_pre * hidden_pre) * 0.3989422804014327
    grad_pre = (grad_act * (cumul + hidden_pre * density)).astype(jnp.bfloat16)
    grad_tokens = jnp.dot(grad_pre, weight_in.T, preferred_element_type=jnp.float32).astype(jnp.bfloat16)
    grad_in = jnp.dot(tokens.T, grad_pre, preferred_element_type=jnp.float32).astype(jnp.bfloat16)
    grad_out = jnp.dot(act.T, out_grad, preferred_element_type=jnp.float32).astype(jnp.bfloat16)
    return block_out, grad_tokens, grad_in, grad_out
```

```python
import functools

import jax
import jax.numpy as jnp
from jax import lax
from jax.sharding import PartitionSpec as P

CHUNKS = 2


def cdf_of(value):
    return 0.5 * (1.0 + lax.erf(value * 0.7071067811865476))


def contract(left, right, left_dim, right_dim):
    return lax.dot_general(
        left, right, (((left_dim,), (right_dim,)), ((), ())), preferred_element_type=jnp.float32
    )


def swap(value, axis, size, mask):
    return lax.ppermute(value, axis, [(i, i ^ mask) for i in range(size)])


def transposed(value, rows, cols):
    per = cols // rows
    pairs = [
        (r * cols + c, (c // per) * cols + r * per + c % per) for r in range(rows) for c in range(cols)
    ]
    return lax.ppermute(value, ("row", "col"), pairs)


def is_small(rows, cols):
    return rows == 4 and cols == 8


def gather_panel(block, rows, cols):
    core = lax.axis_index("row") % 2
    if is_small(rows, cols):
        parts = [block] + [swap(block, "col", cols, 2 * d) for d in (1, 2, 3)]
        mine = jnp.where(
            core == 0,
            jnp.concatenate(parts, axis=1),
            jnp.concatenate(parts[2:] + parts[:2], axis=1),
        )
        other = swap(mine, "col", cols, 1)
        return jnp.where(
            lax.axis_index("col") % 2 == 0,
            jnp.concatenate([mine, other], axis=2),
            jnp.concatenate([other, mine], axis=2),
        )
    per = cols // rows
    two, n, f = block.shape
    whole = lax.all_gather(block, "col", axis=0)
    whole = whole.reshape(rows, per, two, n, f).transpose(2, 0, 3, 1, 4).reshape(two, rows * n, per * f)
    return jnp.where(core == 0, whole, jnp.roll(whole, rows * n // 2, axis=1))


def scatter_sum(terms, rows, cols):
    core = lax.axis_index("row") % 2
    two, all_n, all_f = terms.shape
    n, per = all_n // rows, cols // rows
    f = all_f // per
    if is_small(rows, cols):
        side = lax.axis_index("col") % 2
        away = lax.dynamic_slice_in_dim(terms, (1 - side) * f, f, axis=2).astype(jnp.bfloat16)
        total = lax.dynamic_slice_in_dim(terms, side * f, f, axis=2) + swap(away, "col", cols, 1)

        def block_of(d):
            return lax.dynamic_slice_in_dim(total, (d ^ (2 * core)) * n, n, axis=1)

        out = block_of(0)
        for d in (1, 2, 3):
            out = out + swap(block_of(d).astype(jnp.bfloat16), "col", cols, 2 * d)
        return out
    terms = jnp.where(core == 0, terms, jnp.roll(terms, all_n // 2, axis=1))
    terms = terms.reshape(two, rows, n, per, f).transpose(1, 3, 0, 2, 4).reshape(cols, two, n, f)
    return lax.psum_scatter(terms, "col", scatter_dimension=0)


def body(rows, cols, tokens, weight_in, weight_out, out_grad):
    both = jnp.stack([tokens, out_grad])
    n = tokens.shape[0] // CHUNKS
    panels, acts, pres, outs = [], [], [], []
    for step in range(CHUNKS):
        block = transposed(both[:, step * n : (step + 1) * n], rows, cols)
        panel = gather_panel(block, rows, cols)
        panels.append(panel)
        half = panel.shape[1] // 2
        terms = jnp.stack([contract(panel[0], weight_in, 1, 0), contract(panel[1], weight_out, 1, 1)])
        sums = terms[:, :half] + swap(terms[:, half:].astype(jnp.bfloat16), "row", rows, 1)
        sums = sums + swap(sums.astype(jnp.bfloat16), "row", rows, 2)
        hidden_pre, grad_act = sums[0], sums[1]
        cumul = cdf_of(hidden_pre)
        density = jnp.exp(-0.5 * hidden_pre * hidden_pre) * 0.3989422804014327
        act = (hidden_pre * cumul).astype(jnp.bfloat16)
        grad_pre = (grad_act * (cumul + hidden_pre * density)).astype(jnp.bfloat16)
        own = jnp.stack([act, grad_pre])
        full = jnp.concatenate([own, swap(own, "row", rows, 1)], axis=1)
        acts.append(full[0])
        pres.append(full[1])
        terms = jnp.stack([contract(full[0], weight_out, 1, 0), contract(full[1], weight_in, 1, 1)])
        outs.append(transposed(scatter_sum(terms, rows, cols).astype(jnp.bfloat16), rows, cols))
    panel = jnp.concatenate(panels, axis=1)
    grad_in = contract(panel[0], jnp.concatenate(pres), 0, 0)
    grad_out = contract(jnp.concatenate(acts), panel[1], 0, 0)
    out = jnp.concatenate(outs, axis=1)
    return out[0], out[1], grad_in.astype(jnp.bfloat16), grad_out.astype(jnp.bfloat16)


def solution(mesh):
    return jax.shard_map(
        functools.partial(body, mesh.shape["row"], mesh.shape["col"]),
        mesh=mesh,
        in_specs=(P("row", "col"), P("row", "col"), P("col", "row"), P("row", "col")),
        out_specs=(P("row", "col"), P("row", "col"), P("row", "col"), P("col", "row")),
        check_vma=False,
    )
```

```python
import functools

import jax
import jax.numpy as jnp
from jax import lax
from jax.experimental import pallas as pl
from jax.experimental.pallas import tpu as pltpu
from jax.sharding import PartitionSpec as P

SHARES = (2, 2, 2, 2)
ORDER = (
    0, 1, 0, 1, 0, 2, 1, 0, 2, 3, 1, 2, 0, 2, 0, 3, 1, 3, 2, 1, 3, 0, 2, 0, 3, 1, 0, 3, 1, 0, 2, 0, 1, 2, 1, 3, 1, 3,
    2, -1, 3, 0, 2, 3, 2, 1, 3, -1, 3, 2,
)


def cdf_of(value):
    return 0.5 * (1.0 + lax.erf(value * 0.7071067811865476))


def contract(left, right, left_dim, right_dim):
    return lax.dot_general(
        left, right, (((left_dim,), (right_dim,)), ((), ())), preferred_element_type=jnp.float32
    )


def swap(value, axis, size, mask):
    return lax.ppermute(value, axis, [(i, i ^ mask) for i in range(size)])


def transposed(value, rows, cols):
    per = cols // rows
    pairs = [
        (r * cols + c, (c // per) * cols + r * per + c % per) for r in range(rows) for c in range(cols)
    ]
    return lax.ppermute(value, ("row", "col"), pairs)


def fetch_kernel(*refs):
    count = len(refs) // 2
    copies = [pltpu.make_async_copy(refs[i], refs[count + i], refs[-1].at[i]) for i in range(count)]
    for copy in copies:
        copy.start()
    for copy in copies:
        copy.wait()


def fetched(*arrays):
    size = sum(a.size * a.dtype.itemsize for a in arrays)
    return pl.pallas_call(
        fetch_kernel,
        out_shape=[jax.ShapeDtypeStruct(a.shape, a.dtype) for a in arrays],
        in_specs=[pl.BlockSpec(memory_space=pltpu.HBM)] * len(arrays),
        out_specs=[pl.BlockSpec(memory_space=pltpu.VMEM)] * len(arrays),
        scratch_shapes=[pltpu.SemaphoreType.DMA((len(arrays),))],
        compiler_params=pltpu.CompilerParams(vmem_limit_bytes=size + (2 << 20)),
        cost_estimate=pl.CostEstimate(flops=0, bytes_accessed=2 * size, transcendentals=0),
    )(*arrays)


class Clock:
    def __init__(self, on):
        self.on, self.last = on, None

    def start(self, value):
        if not self.on or self.last is None:
            return value
        return lax.optimization_barrier((value, self.last))[0]

    def end(self, value):
        self.last = value
        return value


class Grid:
    def __init__(self, rows, cols, clock):
        self.rows, self.cols, self.clock = rows, cols, clock
        self.core, self.y = lax.axis_index("row") % 2, lax.axis_index("col") % 2

    def gather(self, block):
        clock = self.clock
        block = clock.end(clock.start(block))
        block = transposed(block, self.rows, self.cols)
        yield
        block = clock.end(clock.start(block))
        far = swap(block, "col", self.cols, 4)
        yield
        near = clock.end(jnp.concatenate([block, clock.start(far)], axis=1))
        far = swap(near, "col", self.cols, 2)
        yield
        far = clock.start(far)
        mine = jnp.where(
            self.core == 0,
            jnp.concatenate([near, far], axis=1),
            jnp.concatenate([far, near], axis=1),
        )
        mine = clock.end(mine)
        other = swap(mine, "col", self.cols, 1)
        yield
        other = clock.start(other)
        return jnp.where(
            self.y == 0,
            jnp.concatenate([mine, other], axis=2),
            jnp.concatenate([other, mine], axis=2),
        )

    def scatter(self, terms):
        clock = self.clock
        f, n = terms.shape[2] // 2, terms.shape[1] // 4
        away = lax.dynamic_slice_in_dim(terms, (1 - self.y) * f, f, axis=2).astype(jnp.bfloat16)
        away = clock.end(away)
        keep = lax.dynamic_slice_in_dim(terms, self.y * f, f, axis=2)
        got = swap(away, "col", self.cols, 1)
        yield
        total = keep + clock.start(got)
        away = lax.dynamic_slice_in_dim(total, (1 - self.core) * 2 * n, 2 * n, axis=1)
        away = clock.end(away.astype(jnp.bfloat16))
        keep = lax.dynamic_slice_in_dim(total, self.core * 2 * n, 2 * n, axis=1)
        got = swap(away, "col", self.cols, 2)
        yield
        total = keep + clock.start(got)
        away = clock.end(total[:, n:].astype(jnp.bfloat16))
        got = swap(away, "col", self.cols, 4)
        yield
        out = clock.end((total[:, :n] + clock.start(got)).astype(jnp.bfloat16))
        out = transposed(out, self.rows, self.cols)
        yield
        return clock.end(clock.start(out))


class Plain:
    def __init__(self, rows, cols, clock):
        self.rows, self.cols, self.per = rows, cols, cols // rows
        self.core = lax.axis_index("row") % 2

    def gather(self, block):
        two, n, f = block.shape
        whole = lax.all_gather(transposed(block, self.rows, self.cols), "col", axis=0)
        yield
        whole = whole.reshape(self.rows, self.per, two, n, f).transpose(2, 0, 3, 1, 4)
        whole = whole.reshape(two, self.rows * n, self.per * f)
        return jnp.where(self.core == 0, whole, jnp.roll(whole, self.rows * n // 2, axis=1))

    def scatter(self, terms):
        two, all_n, all_f = terms.shape
        n, f = all_n // self.rows, all_f // self.per
        terms = jnp.where(self.core == 0, terms, jnp.roll(terms, all_n // 2, axis=1))
        terms = terms.reshape(two, self.rows, n, self.per, f).transpose(1, 3, 0, 2, 4)
        total = lax.psum_scatter(terms.reshape(self.cols, two, n, f), "col", scatter_dimension=0)
        yield
        return transposed(total.astype(jnp.bfloat16), self.rows, self.cols)


def part_steps(grid, clock, rows, weights, block, made):
    panel = yield from grid.gather(block)
    weight_in, weight_out = weights
    half = panel.shape[1] // 2
    terms = jnp.stack([contract(panel[0], weight_in, 1, 0), contract(panel[1], weight_out, 1, 1)])
    away = clock.end(terms[:, half:].astype(jnp.bfloat16))
    got = swap(away, "row", rows, 1)
    yield
    sums = terms[:, :half] + clock.start(got)
    got = swap(clock.end(sums.astype(jnp.bfloat16)), "row", rows, 2)
    yield
    sums = sums + clock.start(got)
    hidden_pre, grad_act = sums[0], sums[1]
    cumul = cdf_of(hidden_pre)
    density = jnp.exp(-0.5 * hidden_pre * hidden_pre) * 0.3989422804014327
    act = (hidden_pre * cumul).astype(jnp.bfloat16)
    grad_pre = (grad_act * (cumul + hidden_pre * density)).astype(jnp.bfloat16)
    own = clock.end(jnp.stack([act, grad_pre]))
    got = swap(own, "row", rows, 1)
    yield
    full = jnp.concatenate([own, clock.start(got)], axis=1)
    made["panel"], made["full"] = panel, full
    terms = jnp.stack([contract(full[0], weight_out, 1, 0), contract(full[1], weight_in, 1, 1)])
    made["out"] = yield from grid.scatter(terms)


def body(rows, cols, tokens, weight_in, weight_out, out_grad):
    special = (rows, cols) == (4, 8)
    clock = Clock(special)
    grid = (Grid if special else Plain)(rows, cols, clock)
    both = jnp.stack([tokens, out_grad])
    weights = [weight_in, weight_out]
    parts, made = [], []
    first = 0
    for share in SHARES:
        n = tokens.shape[0] * share // sum(SHARES)
        made.append({})
        parts.append(part_steps(grid, clock, rows, weights, both[:, first : first + n], made[-1]))
        first += n

    def weight_gradient(of_in):
        panel = jnp.concatenate([m["panel"] for m in made], axis=1)
        full = jnp.concatenate([m["full"] for m in made], axis=1)
        if of_in:
            out = contract(panel[0], clock.start(full[1]), 0, 0)
        else:
            out = contract(clock.start(full[0]), panel[1], 0, 0)
        return clock.end(out.astype(jnp.bfloat16))

    grads = []
    if special:
        for count, part in enumerate(ORDER):
            if count == 1:
                weights[:] = fetched(clock.start(weight_in), weight_out)
                clock.end(weights[1])
            if part < 0:
                grads.append(weight_gradient(not grads))
            else:
                next(parts[part], None)
    else:
        for part in parts:
            for _ in part:
                pass
        grads = [weight_gradient(True), weight_gradient(False)]
    out = jnp.concatenate([m["out"] for m in made], axis=1)
    return out[0], out[1], grads[0], grads[1]


def solution(mesh):
    return jax.shard_map(
        functools.partial(body, mesh.shape["row"], mesh.shape["col"]),
        mesh=mesh,
        in_specs=(P("row", "col"), P("row", "col"), P("col", "row"), P("row", "col")),
        out_specs=(P("row", "col"), P("row", "col"), P("row", "col"), P("col", "row")),
        check_vma=False,
    )
```

```python
import functools

import jax
import jax.numpy as jnp
from jax import lax
from jax.experimental import pallas as pl
from jax.experimental.pallas import tpu as pltpu
from jax.sharding import PartitionSpec as P

LIMIT = 8 << 20
SHARES = (2, 2, 2, 2)
ORDER = (
    0, 1, 0, 1, 0, 2, 1, 0, 2, 3, 1, 2, 0, 2, 0, 3, 1, 3, 2, 1, 3, 0, 2, 0, 3, 1, 0, 3, 1, 0, 2, 0, 1, 2, 1, 3, 1, 3,
    2, -1, 3, 0, 2, 3, 2, 1, 3, -1, 3, 2,
)


VMEM = pl.BlockSpec(memory_space=pltpu.VMEM)
SMEM = pl.BlockSpec(memory_space=pltpu.SMEM)


def cdf_of(value):
    return 0.5 * (1.0 + lax.erf(value * 0.7071067811865476))


def contract(left, right, left_dim, right_dim):
    return lax.dot_general(
        left, right, (((left_dim,), (right_dim,)), ((), ())), preferred_element_type=jnp.float32
    )


def activations(sums):
    hidden_pre, grad_act = sums[0], sums[1]
    cumul = cdf_of(hidden_pre)
    density = jnp.exp(-0.5 * hidden_pre * hidden_pre) * 0.3989422804014327
    act = (hidden_pre * cumul).astype(jnp.bfloat16)
    return act, (grad_act * (cumul + hidden_pre * density)).astype(jnp.bfloat16)


def swap(value, axis, size, mask):
    return lax.ppermute(value, axis, [(i, i ^ mask) for i in range(size)])


def transposed(value, rows, cols):
    per = cols // rows
    pairs = [
        (r * cols + c, (c // per) * cols + r * per + c % per) for r in range(rows) for c in range(cols)
    ]
    return lax.ppermute(value, ("row", "col"), pairs)


def fetch_kernel(*refs):
    count = len(refs) // 2
    copies = [pltpu.make_async_copy(refs[i], refs[count + i], refs[-1].at[i]) for i in range(count)]
    for copy in copies:
        copy.start()
    for copy in copies:
        copy.wait()


def fetched(*arrays):
    return pl.pallas_call(
        fetch_kernel,
        out_shape=[jax.ShapeDtypeStruct(a.shape, a.dtype) for a in arrays],
        in_specs=[pl.BlockSpec(memory_space=pltpu.HBM)] * len(arrays),
        out_specs=[VMEM] * len(arrays),
        scratch_shapes=[pltpu.SemaphoreType.DMA((len(arrays),))],
        compiler_params=pltpu.CompilerParams(vmem_limit_bytes=34 << 20),
    )(*arrays)


def at_part(side, size):
    return pl.multiple_of(side * size, size)


def in_kernel(y_ref, mine, other, weight_in, weight_out, away, keep):
    half, f = mine.shape[1] // 2, mine.shape[2]
    blocks = ((mine, at_part(y_ref[0], f)), (other, at_part(1 - y_ref[0], f)))
    tile = 512

    @pl.loop(0, weight_in.shape[1] // tile)
    def _(step):
        cols = pl.ds(pl.multiple_of(step * tile, tile), tile)
        hidden = [contract(b[0], weight_in[pl.ds(at, f), cols], 1, 0) for b, at in blocks]
        hidden = hidden[0] + hidden[1]
        keep[0, :, cols] = hidden[:half]
        away[0, :, cols] = hidden[half:].astype(away.dtype)
        grad = [contract(b[1], weight_out[cols, pl.ds(at, f)], 1, 1) for b, at in blocks]
        grad = grad[0] + grad[1]
        keep[1, :, cols] = grad[:half]
        away[1, :, cols] = grad[half:].astype(away.dtype)


def out_kernel(y_ref, own, got, weight_in, weight_out, away, keep, full):
    half, f = own.shape[1], keep.shape[2]
    full[:, :half] = own[...]
    full[:, half:] = got[...]
    tile = 256

    @pl.loop(0, f // tile)
    def _(step):
        cols = pl.ds(pl.multiple_of(step * tile, tile), tile)
        for out, side in ((away, 1 - y_ref[0]), (keep, y_ref[0])):
            at = pl.ds(pl.multiple_of(at_part(side, f) + step * tile, tile), tile)
            out[0, :, cols] = contract(full[0], weight_out[:, at], 1, 0).astype(out.dtype)
            out[1, :, cols] = contract(full[1], weight_in[at, :], 1, 1).astype(out.dtype)


def in_terms(y, mine, other, weight_in, weight_out):
    shape = (2, mine.shape[1] // 2, weight_in.shape[1])
    return pl.pallas_call(
        in_kernel,
        out_shape=[jax.ShapeDtypeStruct(shape, jnp.bfloat16), jax.ShapeDtypeStruct(shape, jnp.float32)],
        in_specs=[SMEM, VMEM, VMEM, VMEM, VMEM],
        out_specs=[VMEM, VMEM],
        compiler_params=pltpu.CompilerParams(vmem_limit_bytes=LIMIT),
    )(y, mine, other, weight_in, weight_out)


def out_terms(y, own, got, weight_in, weight_out):
    shape = (2, own.shape[1] * 2, weight_in.shape[0] // 2)
    return pl.pallas_call(
        out_kernel,
        out_shape=[jax.ShapeDtypeStruct(shape, jnp.bfloat16), jax.ShapeDtypeStruct(shape, jnp.float32)],
        in_specs=[SMEM, VMEM, VMEM, VMEM, VMEM],
        out_specs=[VMEM, VMEM],
        scratch_shapes=[pltpu.VMEM((2, own.shape[1] * 2, own.shape[2]), jnp.bfloat16)],
        compiler_params=pltpu.CompilerParams(vmem_limit_bytes=LIMIT),
    )(y, own, got, weight_in, weight_out)


def gradient_kernel(which, parts, y_ref, *refs):
    pieces, (out, tokens, hidden, turned, sems) = refs[: 4 * parts], refs[4 * parts :]
    f = pieces[0].shape[2]
    copies, at = [], 0
    for part in range(parts):
        mine, other, own, got = pieces[4 * part : 4 * part + 4]
        n = mine.shape[1]
        for block, side in ((mine, y_ref[0]), (other, 1 - y_ref[0])):
            copies.append((block.at[1 - which], tokens.at[pl.ds(at, n), pl.ds(at_part(side, f), f)]))
        for block in (own, got):
            copies.append((block.at[which], hidden.at[pl.ds(at, n // 2)]))
            at += n // 2

    @pl.when(pl.program_id(0) == 0)
    def _():
        started = [pltpu.make_async_copy(*copy, sems.at[i]) for i, copy in enumerate(copies)]
        for copy in started:
            copy.start()
        for copy in started:
            copy.wait()

    left, right = (tokens, hidden) if which else (hidden, tokens)
    rows = out.shape[0]
    cols = pl.ds(pl.multiple_of(pl.program_id(0) * rows, rows), rows)
    turned[...] = left[:, cols].T
    tile = 512

    @pl.loop(0, out.shape[1] // tile)
    def _(step):
        at = pl.ds(pl.multiple_of(step * tile, tile), tile)
        out[:, at] = contract(turned[...], right[:, at], 1, 0).astype(out.dtype)


def weight_gradient(which, y, made):
    pieces = [piece for part in made for piece in part["pieces"]]
    rows = sum(part["pieces"][0].shape[1] for part in made)
    width, ff = 2 * pieces[0].shape[2], pieces[2].shape[2]
    shape = (width, ff) if which else (ff, width)
    tile = 256 if which else 512
    return pl.pallas_call(
        functools.partial(gradient_kernel, which, len(made)),
        out_shape=jax.ShapeDtypeStruct(shape, jnp.bfloat16),
        grid=(shape[0] // tile,),
        in_specs=[SMEM] + [pl.BlockSpec(memory_space=pl.ANY)] * len(pieces),
        out_specs=pl.BlockSpec((tile, shape[1]), lambda i: (i, 0)),
        scratch_shapes=[
            pltpu.VMEM((rows, width), jnp.bfloat16),
            pltpu.VMEM((rows, ff), jnp.bfloat16),
            pltpu.VMEM((tile, rows), jnp.bfloat16),
            pltpu.SemaphoreType.DMA((len(pieces),)),
        ],
        compiler_params=pltpu.CompilerParams(vmem_limit_bytes=24 << 20),
    )(y, *pieces)


class Clock:
    def __init__(self):
        self.last = None

    def start(self, value):
        if self.last is None:
            return value
        return lax.optimization_barrier((value, self.last))[0]

    def end(self, value):
        self.last = value
        return value


class Grid:
    def __init__(self, rows, cols, clock):
        self.rows, self.cols, self.clock = rows, cols, clock
        self.core = lax.axis_index("row") % 2
        self.side = jnp.reshape(lax.axis_index("col") % 2, (1,)).astype(jnp.int32)

    def gather(self, block):
        clock = self.clock
        block = clock.end(clock.start(block))
        block = transposed(block, self.rows, self.cols)
        yield
        block = clock.end(clock.start(block))
        far = swap(block, "col", self.cols, 4)
        yield
        near = clock.end(jnp.concatenate([block, clock.start(far)], axis=1))
        far = swap(near, "col", self.cols, 2)
        yield
        far = clock.start(far)
        mine = jnp.where(
            self.core == 0,
            jnp.concatenate([near, far], axis=1),
            jnp.concatenate([far, near], axis=1),
        )
        mine = clock.end(mine)
        other = swap(mine, "col", self.cols, 1)
        yield
        return mine, clock.start(other)

    def scatter(self, away, keep):
        clock, n = self.clock, keep.shape[1] // 4
        clock.end(away)
        got = swap(away, "col", self.cols, 1)
        yield
        total = keep + clock.start(got)
        away = lax.dynamic_slice_in_dim(total, (1 - self.core) * 2 * n, 2 * n, axis=1)
        away = clock.end(away.astype(jnp.bfloat16))
        keep = lax.dynamic_slice_in_dim(total, self.core * 2 * n, 2 * n, axis=1)
        got = swap(away, "col", self.cols, 2)
        yield
        total = keep + clock.start(got)
        away = clock.end(total[:, n:].astype(jnp.bfloat16))
        got = swap(away, "col", self.cols, 4)
        yield
        out = clock.end((total[:, :n] + clock.start(got)).astype(jnp.bfloat16))
        out = transposed(out, self.rows, self.cols)
        yield
        return clock.end(clock.start(out))


def part_steps(grid, clock, weights, block, made):
    rows = grid.rows
    mine, other = yield from grid.gather(block)
    away, keep = in_terms(grid.side, mine, other, *weights)
    got = swap(clock.end(away), "row", rows, 1)
    yield
    sums = keep + clock.start(got)
    got = swap(clock.end(sums.astype(jnp.bfloat16)), "row", rows, 2)
    yield
    act, grad_pre = activations(sums + clock.start(got))
    own = clock.end(jnp.stack([act, grad_pre]))
    got = swap(own, "row", rows, 1)
    yield
    got = clock.start(got)
    made["pieces"] = mine, other, own, got
    made["out"] = yield from grid.scatter(*out_terms(grid.side, own, got, *weights))


def body(rows, cols, tokens, weight_in, weight_out, out_grad):
    clock = Clock()
    grid = Grid(rows, cols, clock)
    both = jnp.stack([tokens, out_grad])
    weights = [weight_in, weight_out]
    parts, made = [], []
    first = 0
    for share in SHARES:
        n = tokens.shape[0] * share // sum(SHARES)
        made.append({})
        parts.append(part_steps(grid, clock, weights, both[:, first : first + n], made[-1]))
        first += n
    grads = []
    for count, part in enumerate(ORDER):
        if count == 1:
            weights[:] = fetched(clock.start(weight_in), weight_out)
            clock.end(weights[1])
        if part < 0:
            made[0]["pieces"] = (clock.start(made[0]["pieces"][0]), *made[0]["pieces"][1:])
            grads.append(clock.end(weight_gradient(1 - len(grads), grid.side, made)))
        else:
            next(parts[part], None)
    out = jnp.concatenate([m["out"] for m in made], axis=1)
    return out[0], out[1], grads[0], grads[1]


def plain_body(rows, cols, tokens, weight_in, weight_out, out_grad):
    per = cols // rows
    both = jnp.stack([tokens, out_grad])
    two, n, f = both.shape
    panel = lax.all_gather(transposed(both, rows, cols), "col", axis=0)
    panel = panel.reshape(rows, per, two, n, f).transpose(2, 0, 3, 1, 4).reshape(two, rows * n, per * f)
    terms = jnp.stack([contract(panel[0], weight_in, 1, 0), contract(panel[1], weight_out, 1, 1)])
    act, grad_pre = activations(lax.psum_scatter(terms, "row", scatter_dimension=1, tiled=True))
    full = lax.all_gather(jnp.stack([act, grad_pre]), "row", axis=1, tiled=True)
    terms = jnp.stack([contract(full[0], weight_out, 1, 0), contract(full[1], weight_in, 1, 1)])
    terms = terms.reshape(two, rows, n, per, f).transpose(1, 3, 0, 2, 4).reshape(cols, two, n, f)
    out = lax.psum_scatter(terms, "col", scatter_dimension=0).astype(jnp.bfloat16)
    out = transposed(out, rows, cols)
    grad_in = contract(panel[0], full[1], 0, 0).astype(jnp.bfloat16)
    grad_out = contract(full[0], panel[1], 0, 0).astype(jnp.bfloat16)
    return out[0], out[1], grad_in, grad_out


def solution(mesh):
    shape = (mesh.shape["row"], mesh.shape["col"])
    return jax.shard_map(
        functools.partial(body if shape == (4, 8) else plain_body, *shape),
        mesh=mesh,
        in_specs=(P("row", "col"), P("row", "col"), P("col", "row"), P("row", "col")),
        out_specs=(P("row", "col"), P("row", "col"), P("row", "col"), P("col", "row")),
        check_vma=False,
    )
```

```python
import functools

import jax
import jax.numpy as jnp
from jax import lax
from jax.experimental import pallas as pl
from jax.experimental.pallas import tpu as pltpu
from jax.sharding import PartitionSpec as P

LIMIT = 48 << 20

SHARES = (2, 2, 2, 2)
ORDER = (
    0, 0, 1, 0, 1, 0, 1, 2, 0, 1, 2, 0, 2, 3, 1, 2, 3, 1, 3, 0, 2, 3, 0, 2, 1, 3, 0, 1, 3, 2,
    0, 1, 2, 0, 1, 3, 2, 3, 1, 2, -1, 3, 2, 3, 3, -1, 0, 1, 2, 3,
)


VMEM = pl.BlockSpec(memory_space=pltpu.VMEM)
SMEM = pl.BlockSpec(memory_space=pltpu.SMEM)
HBM = pl.BlockSpec(memory_space=pltpu.HBM)


def cdf_of(value):
    return 0.5 * (1.0 + lax.erf(value * 0.7071067811865476))


def contract(left, right, left_dim, right_dim):
    return lax.dot_general(
        left, right, (((left_dim,), (right_dim,)), ((), ())), preferred_element_type=jnp.float32
    )


def activations(sums):
    hidden_pre, grad_act = sums[0], sums[1]
    cumul = cdf_of(hidden_pre)
    density = jnp.exp(-0.5 * hidden_pre * hidden_pre) * 0.3989422804014327
    act = (hidden_pre * cumul).astype(jnp.bfloat16)
    return act, (grad_act * (cumul + hidden_pre * density)).astype(jnp.bfloat16)


def swap(value, axis, size, mask):
    return lax.ppermute(value, axis, [(i, i ^ mask) for i in range(size)])


def transposed(value, rows, cols):
    per = cols // rows
    pairs = [
        (r * cols + c, (c // per) * cols + r * per + c % per) for r in range(rows) for c in range(cols)
    ]
    return lax.ppermute(value, ("row", "col"), pairs)


def streamed(sources, slots, sems, count, use):
    depth = slots[0].shape[0]

    def copies(j):
        return [
            pltpu.make_async_copy(source(j), slot.at[j % depth], sems.at[i, j % depth])
            for i, (source, slot) in enumerate(zip(sources, slots))
        ]

    for j in range(min(depth - 1, count)):
        for copy in copies(j):
            copy.start()
    for j in range(count):
        if j + depth - 1 < count:
            for copy in copies(j + depth - 1):
                copy.start()
        for copy in copies(j):
            copy.wait()
        use(j, j % depth)


def kept(sems, *pairs):
    copies = [pltpu.make_async_copy(*pair, sems.at[i]) for i, pair in enumerate(pairs)]
    for copy in copies:
        copy.start()
    return copies


def in_kernel(first, at_ref, mine, other, weight_in, weight_out, *refs):
    away, keep, tok_all, grad_all, panel, in_slots, out_slots, sems, keep_sems = refs[-9:]
    half, f = keep.shape[1], panel.shape[2] // 2
    side = at_ref[0]
    panel[:, :, pl.ds(pl.multiple_of(side * f, f), f)] = mine[...]
    panel[:, :, pl.ds(pl.multiple_of((1 - side) * f, f), f)] = other[...]
    rows = pl.ds(first, 2 * half)
    stored = kept(keep_sems, (panel.at[0], tok_all.at[rows]), (panel.at[1], grad_all.at[rows]))
    tile = in_slots.shape[2]

    def use(j, slot):
        cols = slice(j * tile, (j + 1) * tile)
        hidden = contract(panel[0], in_slots[slot], 1, 0)
        keep[0, :, cols] = hidden[:half]
        away[0, :, cols] = hidden[half:].astype(away.dtype)
        grad = contract(panel[1], out_slots[slot], 1, 1)
        keep[1, :, cols] = grad[:half]
        away[1, :, cols] = grad[half:].astype(away.dtype)

    streamed(
        [lambda j: weight_in.at[:, pl.ds(j * tile, tile)], lambda j: weight_out.at[pl.ds(j * tile, tile)]],
        [in_slots, out_slots],
        sems,
        weight_in.shape[1] // tile,
        use,
    )
    for copy in stored:
        copy.wait()


def out_kernel(first, at_ref, own, got, weight_in, weight_out, *refs):
    away, keep, act_all, pre_all, full, in_slots, out_slots, sems, keep_sems = refs[-9:]
    half, f = own.shape[1], keep.shape[2]
    full[:, :half] = own[...]
    full[:, half:] = got[...]
    rows = pl.ds(first, 2 * half)
    stored = kept(keep_sems, (full.at[0], act_all.at[rows]), (full.at[1], pre_all.at[rows]))
    tile = in_slots.shape[1]
    per = f // tile
    side = at_ref[0]

    def at(j):
        block = side if j >= per else 1 - side
        return pl.ds(pl.multiple_of(block * f + (j % per) * tile, tile), tile)

    def use(j, slot):
        out = keep if j >= per else away
        cols = slice((j % per) * tile, (j % per + 1) * tile)
        out[0, :, cols] = contract(full[0], out_slots[slot], 1, 0).astype(out.dtype)
        out[1, :, cols] = contract(full[1], in_slots[slot], 1, 1).astype(out.dtype)

    streamed(
        [lambda j: weight_in.at[at(j)], lambda j: weight_out.at[:, at(j)]],
        [in_slots, out_slots],
        sems,
        2 * per,
        use,
    )
    for copy in stored:
        copy.wait()


def terms_call(kernel, at, blocks, weights, all_arrays, total, shape, panel_shape, slots):
    inputs = [at, *blocks, *weights]
    specs = [SMEM] + [VMEM] * len(blocks) + [HBM] * len(weights)
    aliases = {}
    if all_arrays is not None:
        aliases = {len(inputs): 2, len(inputs) + 1: 3}
        inputs += all_arrays
        specs += [HBM] * 2
    kept_shape = jax.ShapeDtypeStruct((total, panel_shape[2]), jnp.bfloat16)
    away, keep, *all_arrays = pl.pallas_call(
        kernel,
        out_shape=[
            jax.ShapeDtypeStruct(shape, jnp.bfloat16),
            jax.ShapeDtypeStruct(shape, jnp.float32),
            kept_shape,
            kept_shape,
        ],
        in_specs=specs,
        out_specs=[VMEM, VMEM, HBM, HBM],
        scratch_shapes=[
            pltpu.VMEM(panel_shape, jnp.bfloat16),
            *[pltpu.VMEM(slot, jnp.bfloat16) for slot in slots],
            pltpu.SemaphoreType.DMA((2, slots[0][0])),
            pltpu.SemaphoreType.DMA((2,)),
        ],
        input_output_aliases=aliases,
        compiler_params=pltpu.CompilerParams(vmem_limit_bytes=LIMIT),
    )(*inputs)
    return away, keep, all_arrays


def in_terms(at, blocks, weights, kept_arrays, first, n, total):
    width, ff = weights[0].shape
    return terms_call(
        functools.partial(in_kernel, first),
        at,
        blocks,
        weights,
        kept_arrays,
        total,
        (2, 2 * n, ff),
        (2, 4 * n, width),
        [(3, width, 512), (3, 512, width)],
    )


def out_terms(at, own, got, weights, kept_arrays, first, total):
    width, ff = weights[0].shape
    n = own.shape[1]
    return terms_call(
        functools.partial(out_kernel, first),
        at,
        (own, got),
        weights,
        kept_arrays,
        total,
        (2, 2 * n, width // 2),
        (2, 2 * n, ff),
        [(3, 256, ff), (3, ff, 256)],
    )


class Clock:
    def __init__(self):
        self.last = None

    def start(self, value):
        if self.last is None:
            return value
        return lax.optimization_barrier((value, self.last))[0]

    def end(self, value):
        self.last = value
        return value


class Grid:
    def __init__(self, rows, cols, clock):
        self.rows, self.cols, self.clock = rows, cols, clock
        self.core = lax.axis_index("row") % 2
        self.at = jnp.reshape(lax.axis_index("col") % 2, (1,)).astype(jnp.int32)

    def gather(self, block):
        clock = self.clock
        block = transposed(clock.end(clock.start(block)), self.rows, self.cols)
        yield
        block = clock.end(clock.start(block))
        far = swap(block, "col", self.cols, 4)
        yield
        near = clock.end(jnp.concatenate([block, clock.start(far)], axis=1))
        far = swap(near, "col", self.cols, 2)
        yield
        far = clock.start(far)
        mine = jnp.where(
            self.core == 0,
            jnp.concatenate([near, far], axis=1),
            jnp.concatenate([far, near], axis=1),
        )
        mine = clock.end(mine)
        other = swap(mine, "col", self.cols, 1)
        yield
        return mine, clock.start(other)

    def scatter(self, away, keep):
        clock, n = self.clock, keep.shape[1] // 4
        clock.end(away)
        got = swap(away, "col", self.cols, 1)
        yield
        total = keep + clock.start(got)
        away = lax.dynamic_slice_in_dim(total, (1 - self.core) * 2 * n, 2 * n, axis=1)
        away = clock.end(away.astype(jnp.bfloat16))
        keep = lax.dynamic_slice_in_dim(total, self.core * 2 * n, 2 * n, axis=1)
        got = swap(away, "col", self.cols, 2)
        yield
        total = keep + clock.start(got)
        away = clock.end(total[:, n:].astype(jnp.bfloat16))
        got = swap(away, "col", self.cols, 4)
        yield
        out = clock.end((total[:, :n] + clock.start(got)).astype(jnp.bfloat16))
        out = transposed(out, self.rows, self.cols)
        yield
        return clock.end(clock.start(out))


def part_steps(grid, block, weights, kept_arrays, first, total):
    clock, rows, n = grid.clock, grid.rows, block.shape[1]
    blocks = yield from grid.gather(block)
    away, keep, kept_arrays["tokens"] = in_terms(
        grid.at, blocks, weights, kept_arrays.get("tokens"), first, n, total
    )
    got = swap(clock.end(away), "row", rows, 1)
    yield
    sums = keep + clock.start(got)
    got = swap(clock.end(sums.astype(jnp.bfloat16)), "row", rows, 2)
    yield
    act, grad_pre = activations(sums + clock.start(got))
    own = clock.end(jnp.stack([act, grad_pre]))
    got = swap(own, "row", rows, 1)
    yield
    away, keep, kept_arrays["hidden"] = out_terms(
        grid.at, own, clock.start(got), weights, kept_arrays.get("hidden"), first, total
    )
    return (yield from grid.scatter(away, keep))


def body(rows, cols, tokens, weight_in, weight_out, out_grad):
    clock = Clock()
    grid = Grid(rows, cols, clock)
    both = jnp.stack([tokens, out_grad])
    count = tokens.shape[0]
    size = [count * share // sum(SHARES) for share in SHARES]
    outs, kept_arrays = [None] * len(size), {}

    def run(part):
        first = sum(size[:part])
        outs[part] = yield from part_steps(
            grid,
            both[:, first : first + size[part]],
            (weight_in, weight_out),
            kept_arrays,
            rows * first,
            rows * count,
        )

    parts = [run(part) for part in range(len(size))]
    grads = []
    for part in ORDER:
        if part >= 0:
            next(parts[part], None)
            continue
        panel, full = kept_arrays["tokens"][len(grads)], kept_arrays["hidden"][1 - len(grads)]
        full = clock.start(full)
        grad = contract(full, panel, 0, 0) if grads else contract(panel, full, 0, 0)
        grads.append(clock.end(grad.astype(jnp.bfloat16)))
    out = jnp.concatenate(outs, axis=1)
    return out[0], out[1], grads[0], grads[1]


def plain_body(rows, cols, tokens, weight_in, weight_out, out_grad):
    per = cols // rows
    both = jnp.stack([tokens, out_grad])
    two, n, f = both.shape
    panel = lax.all_gather(transposed(both, rows, cols), "col", axis=0)
    panel = panel.reshape(rows, per, two, n, f).transpose(2, 0, 3, 1, 4).reshape(two, rows * n, per * f)
    terms = jnp.stack([contract(panel[0], weight_in, 1, 0), contract(panel[1], weight_out, 1, 1)])
    act, grad_pre = activations(lax.psum_scatter(terms, "row", scatter_dimension=1, tiled=True))
    full = lax.all_gather(jnp.stack([act, grad_pre]), "row", axis=1, tiled=True)
    terms = jnp.stack([contract(full[0], weight_out, 1, 0), contract(full[1], weight_in, 1, 1)])
    terms = terms.reshape(two, rows, n, per, f).transpose(1, 3, 0, 2, 4).reshape(cols, two, n, f)
    out = lax.psum_scatter(terms, "col", scatter_dimension=0).astype(jnp.bfloat16)
    out = transposed(out, rows, cols)
    grad_in = contract(panel[0], full[1], 0, 0).astype(jnp.bfloat16)
    grad_out = contract(full[0], panel[1], 0, 0).astype(jnp.bfloat16)
    return out[0], out[1], grad_in, grad_out


def solution(mesh):
    shape = (mesh.shape["row"], mesh.shape["col"])
    return jax.shard_map(
        functools.partial(body if shape == (4, 8) else plain_body, *shape),
        mesh=mesh,
        in_specs=(P("row", "col"), P("row", "col"), P("col", "row"), P("row", "col")),
        out_specs=(P("row", "col"), P("row", "col"), P("row", "col"), P("col", "row")),
        check_vma=False,
    )
```

```python
import functools

import jax
import jax.numpy as jnp
from jax import lax
from jax.experimental import pallas as pl
from jax.experimental.pallas import tpu as pltpu
from jax.sharding import PartitionSpec as P

SHARES = (3, 3, 2)
ORDER = (
    0, 0, 1, 0, 1, 0, 1, 2, 0, 1, 0, 2, 2, 1, 0, 2, 1, 2, 0, 2, 3, 1, 0, 1, 4, 0, 2, 1, 0, 2,
    5, 1, -1, 2, 1, 2, -1, 2, 0, 1, 2,
)


HBM = pl.BlockSpec(memory_space=pltpu.HBM)


def cdf_of(value):
    return 0.5 * (1.0 + lax.erf(value * 0.7071067811865476))


def contract(left, right, left_dim, right_dim):
    return lax.dot_general(
        left, right, (((left_dim,), (right_dim,)), ((), ())), preferred_element_type=jnp.float32
    )


def activations(sums):
    hidden_pre, grad_act = sums[0], sums[1]
    cumul = cdf_of(hidden_pre)
    density = jnp.exp(-0.5 * hidden_pre * hidden_pre) * 0.3989422804014327
    act = (hidden_pre * cumul).astype(jnp.bfloat16)
    return act, (grad_act * (cumul + hidden_pre * density)).astype(jnp.bfloat16)


def swap(value, axis, size, mask):
    return lax.ppermute(value, axis, [(i, i ^ mask) for i in range(size)])


def transposed(value, rows, cols):
    per = cols // rows
    pairs = [
        (r * cols + c, (c // per) * cols + r * per + c % per) for r in range(rows) for c in range(cols)
    ]
    return lax.ppermute(value, ("row", "col"), pairs)


def store_kernel(first, full, panel, *refs):
    arrays, sems = refs[-5:-1], refs[-1]
    rows = pl.ds(first, full.shape[1])
    sources = (panel.at[0], panel.at[1], full.at[0], full.at[1])
    copies = [
        pltpu.make_async_copy(source, array.at[rows], sems.at[i])
        for i, (source, array) in enumerate(zip(sources, arrays))
    ]
    for copy in copies:
        copy.start()
    for copy in copies:
        copy.wait()


def stored(full, panel, arrays, first, total):
    inputs = [full, panel, *(arrays or ())]
    shapes = [jax.ShapeDtypeStruct((total, a.shape[2]), jnp.bfloat16) for a in (panel, panel, full, full)]
    return pl.pallas_call(
        functools.partial(store_kernel, first),
        out_shape=shapes,
        in_specs=[pl.BlockSpec(memory_space=pl.ANY)] * len(inputs),
        out_specs=[HBM] * 4,
        scratch_shapes=[pltpu.SemaphoreType.DMA((4,))],
        input_output_aliases={2 + i: i for i in range(4)} if arrays else {},
        cost_estimate=pl.CostEstimate(flops=0, bytes_accessed=4 * full.size, transcendentals=0),
    )(*inputs)


class Clock:
    def __init__(self):
        self.last = None

    def start(self, value):
        if self.last is None:
            return value
        return lax.optimization_barrier((value, self.last))[0]

    def end(self, value):
        self.last = value
        return value


class Grid:
    def __init__(self, rows, cols, clock):
        self.rows, self.cols, self.clock = rows, cols, clock
        self.core = lax.axis_index("row") % 2
        self.y = lax.axis_index("col") % 2

    def gather(self, block):
        clock = self.clock
        block = transposed(clock.end(clock.start(block)), self.rows, self.cols)
        yield
        block = clock.end(clock.start(block))
        far = swap(block, "col", self.cols, 4)
        yield
        near = clock.end(jnp.concatenate([block, clock.start(far)], axis=1))
        far = swap(near, "col", self.cols, 2)
        yield
        far = clock.start(far)
        mine = jnp.where(
            self.core == 0,
            jnp.concatenate([near, far], axis=1),
            jnp.concatenate([far, near], axis=1),
        )
        mine = clock.end(mine)
        other = swap(mine, "col", self.cols, 1)
        yield
        other = clock.start(other)
        return jnp.where(
            self.y == 0,
            jnp.concatenate([mine, other], axis=2),
            jnp.concatenate([other, mine], axis=2),
        )

    def scatter(self, terms):
        clock = self.clock
        f, n = terms.shape[2] // 2, terms.shape[1] // 4
        away = lax.dynamic_slice_in_dim(terms, (1 - self.y) * f, f, axis=2).astype(jnp.bfloat16)
        away = clock.end(away)
        keep = lax.dynamic_slice_in_dim(terms, self.y * f, f, axis=2)
        got = swap(away, "col", self.cols, 1)
        yield
        total = keep + clock.start(got)
        away = lax.dynamic_slice_in_dim(total, (1 - self.core) * 2 * n, 2 * n, axis=1)
        away = clock.end(away.astype(jnp.bfloat16))
        keep = lax.dynamic_slice_in_dim(total, self.core * 2 * n, 2 * n, axis=1)
        got = swap(away, "col", self.cols, 2)
        yield
        total = keep + clock.start(got)
        away = clock.end(total[:, n:].astype(jnp.bfloat16))
        got = swap(away, "col", self.cols, 4)
        yield
        out = clock.end((total[:, :n] + clock.start(got)).astype(jnp.bfloat16))
        out = transposed(out, self.rows, self.cols)
        yield
        return clock.end(clock.start(out))


def part_steps(grid, block, weights, made):
    clock, rows = grid.clock, grid.rows
    weight_in, weight_out = weights
    panel = yield from grid.gather(block)
    half = panel.shape[1] // 2
    terms = jnp.stack([contract(panel[0], weight_in, 1, 0), contract(panel[1], weight_out, 1, 1)])
    away = clock.end(terms[:, half:].astype(jnp.bfloat16))
    got = swap(away, "row", rows, 1)
    yield
    sums = terms[:, :half] + clock.start(got)
    got = swap(clock.end(sums.astype(jnp.bfloat16)), "row", rows, 2)
    yield
    act, grad_pre = activations(sums + clock.start(got))
    own = clock.end(jnp.stack([act, grad_pre]))
    got = swap(own, "row", rows, 1)
    yield
    full = jnp.concatenate([own, clock.start(got)], axis=1)
    made["operands"] = full, panel
    terms = jnp.stack([contract(full[0], weight_out, 1, 0), contract(full[1], weight_in, 1, 1)])
    made["out"] = yield from grid.scatter(terms)


def body(rows, cols, tokens, weight_in, weight_out, out_grad):
    clock = Clock()
    grid = Grid(rows, cols, clock)
    both = jnp.stack([tokens, out_grad])
    count = tokens.shape[0]
    size = [count * share // sum(SHARES) for share in SHARES]
    start = [sum(size[:part]) for part in range(len(size))]
    made = [{} for _ in size]
    parts = [
        part_steps(grid, both[:, at : at + n], (weight_in, weight_out), out)
        for at, n, out in zip(start, size, made)
    ]
    arrays, grads = None, []
    for part in ORDER:
        if part < 0:
            panel, full = arrays[len(grads)], clock.start(arrays[3 - len(grads)])
            grad = contract(full, panel, 0, 0) if grads else contract(panel, full, 0, 0)
            grads.append(clock.end(grad.astype(jnp.bfloat16)))
        elif part >= len(parts):
            full, panel = made[part - len(parts)]["operands"]
            arrays = stored(clock.start(full), panel, arrays, rows * start[part - len(parts)], rows * count)
            clock.end(arrays[3])
        else:
            next(parts[part], None)
    out = jnp.concatenate([m["out"] for m in made], axis=1)
    return out[0], out[1], grads[0], grads[1]


def plain_body(rows, cols, tokens, weight_in, weight_out, out_grad):
    per = cols // rows
    both = jnp.stack([tokens, out_grad])
    two, n, f = both.shape
    panel = lax.all_gather(transposed(both, rows, cols), "col", axis=0)
    panel = panel.reshape(rows, per, two, n, f).transpose(2, 0, 3, 1, 4).reshape(two, rows * n, per * f)
    terms = jnp.stack([contract(panel[0], weight_in, 1, 0), contract(panel[1], weight_out, 1, 1)])
    act, grad_pre = activations(lax.psum_scatter(terms, "row", scatter_dimension=1, tiled=True))
    full = lax.all_gather(jnp.stack([act, grad_pre]), "row", axis=1, tiled=True)
    terms = jnp.stack([contract(full[0], weight_out, 1, 0), contract(full[1], weight_in, 1, 1)])
    terms = terms.reshape(two, rows, n, per, f).transpose(1, 3, 0, 2, 4).reshape(cols, two, n, f)
    out = lax.psum_scatter(terms, "col", scatter_dimension=0).astype(jnp.bfloat16)
    out = transposed(out, rows, cols)
    grad_in = contract(panel[0], full[1], 0, 0).astype(jnp.bfloat16)
    grad_out = contract(full[0], panel[1], 0, 0).astype(jnp.bfloat16)
    return out[0], out[1], grad_in, grad_out


def solution(mesh):
    shape = (mesh.shape["row"], mesh.shape["col"])
    return jax.shard_map(
        functools.partial(body if shape == (4, 8) else plain_body, *shape),
        mesh=mesh,
        in_specs=(P("row", "col"), P("row", "col"), P("col", "row"), P("row", "col")),
        out_specs=(P("row", "col"), P("row", "col"), P("row", "col"), P("col", "row")),
        check_vma=False,
    )
```

```python
import functools

import jax
import jax.numpy as jnp
from jax import lax
from jax.experimental import pallas as pl
from jax.experimental.pallas import tpu as pltpu
from jax.sharding import PartitionSpec as P

LIMIT = 6 << 20
STREAM_LIMIT = 48 << 20
COST = 10**9

SHARES = (2, 2, 2, 2)
ORDER = (
    0, 0, 1, 0, 1, 0, 1, 2, 0, 1, 2, 0, 2, 3, 1, 0, 2, 1, 3, 0, 2, 3, 1, 2, 3, 0, 1, 3, 2, 0,
    3, 1, 2, 0, 1, 3, 2, 3, 1, 2, -1, 3, 2, 3, 3, -1, 0, 1, 2, 3,
)


VMEM = pl.BlockSpec(memory_space=pltpu.VMEM)
SMEM = pl.BlockSpec(memory_space=pltpu.SMEM)
HBM = pl.BlockSpec(memory_space=pltpu.HBM)


def cdf_of(value):
    return 0.5 * (1.0 + lax.erf(value * 0.7071067811865476))


def contract(left, right, left_dim, right_dim):
    return lax.dot_general(
        left, right, (((left_dim,), (right_dim,)), ((), ())), preferred_element_type=jnp.float32
    )


def activations(sums):
    hidden_pre, grad_act = sums[0], sums[1]
    cumul = cdf_of(hidden_pre)
    density = jnp.exp(-0.5 * hidden_pre * hidden_pre) * 0.3989422804014327
    act = (hidden_pre * cumul).astype(jnp.bfloat16)
    return act, (grad_act * (cumul + hidden_pre * density)).astype(jnp.bfloat16)


def swap(value, axis, size, mask):
    return lax.ppermute(value, axis, [(i, i ^ mask) for i in range(size)])


def transposed(value, rows, cols):
    per = cols // rows
    pairs = [
        (r * cols + c, (c // per) * cols + r * per + c % per) for r in range(rows) for c in range(cols)
    ]
    return lax.ppermute(value, ("row", "col"), pairs)


def streamed(sources, slots, sems, count, use):
    depth = slots[0].shape[0]

    def copies(j):
        return [
            pltpu.make_async_copy(source(j), slot.at[j % depth], sems.at[i, j % depth])
            for i, (source, slot) in enumerate(zip(sources, slots))
        ]

    for j in range(min(depth - 1, count)):
        for copy in copies(j):
            copy.start()
    for j in range(count):
        if j + depth - 1 < count:
            for copy in copies(j + depth - 1):
                copy.start()
        for copy in copies(j):
            copy.wait()
        use(j, j % depth)


def kept(sems, *pairs):
    copies = [pltpu.make_async_copy(*pair, sems.at[i]) for i, pair in enumerate(pairs)]
    for copy in copies:
        copy.start()
    return copies


def in_kernel(first, stream, at_ref, mine, other, weight_in, weight_out, *refs):
    away, keep, tok_all, grad_all, panel, keep_sems, *streaming = refs[-9:] if stream else refs[-6:]
    half, f = keep.shape[1], panel.shape[2] // 2
    side = at_ref[0]
    panel[:, :, pl.ds(pl.multiple_of(side * f, f), f)] = mine[...]
    panel[:, :, pl.ds(pl.multiple_of((1 - side) * f, f), f)] = other[...]
    rows = pl.ds(first, 2 * half)
    copies = kept(keep_sems, (panel.at[0], tok_all.at[rows]), (panel.at[1], grad_all.at[rows]))
    tile = 512

    def use(j, in_tile, out_tile):
        cols = slice(j * tile, (j + 1) * tile)
        hidden = contract(panel[0], in_tile, 1, 0)
        keep[0, :, cols] = hidden[:half]
        away[0, :, cols] = hidden[half:].astype(away.dtype)
        grad = contract(panel[1], out_tile, 1, 1)
        keep[1, :, cols] = grad[:half]
        away[1, :, cols] = grad[half:].astype(away.dtype)

    count = weight_in.shape[1] // tile
    if stream:
        in_slots, out_slots, sems = streaming
        streamed(
            [lambda j: weight_in.at[:, pl.ds(j * tile, tile)], lambda j: weight_out.at[pl.ds(j * tile, tile)]],
            [in_slots, out_slots],
            sems,
            count,
            lambda j, slot: use(j, in_slots[slot], out_slots[slot]),
        )
    else:
        for j in range(count):
            cols = slice(j * tile, (j + 1) * tile)
            use(j, weight_in[:, cols], weight_out[cols])
    for copy in copies:
        copy.wait()


def out_kernel(first, at_ref, own, got, weight_in, weight_out, *refs):
    away, keep, act_all, pre_all, full, keep_sems = refs[-6:]
    half, f = own.shape[1], keep.shape[2]
    full[:, :half] = own[...]
    full[:, half:] = got[...]
    rows = pl.ds(first, 2 * half)
    copies = kept(keep_sems, (full.at[0], act_all.at[rows]), (full.at[1], pre_all.at[rows]))
    tile = 256
    for out, side in ((away, 1 - at_ref[0]), (keep, at_ref[0])):
        for j in range(f // tile):
            cols = slice(j * tile, (j + 1) * tile)
            at = pl.ds(pl.multiple_of(side * f + j * tile, tile), tile)
            out[0, :, cols] = contract(full[0], weight_out[:, at], 1, 0).astype(out.dtype)
            out[1, :, cols] = contract(full[1], weight_in[at, :], 1, 1).astype(out.dtype)
    for copy in copies:
        copy.wait()


def terms_call(kernel, at, blocks, weights, all_arrays, total, shape, panel_shape, slots=()):
    inputs = [at, *blocks, *weights]
    specs = [SMEM] + [VMEM] * len(blocks) + [HBM if slots else VMEM] * len(weights)
    aliases = {}
    if all_arrays is not None:
        aliases = {len(inputs): 2, len(inputs) + 1: 3}
        inputs += all_arrays
        specs += [HBM] * 2
    kept_shape = jax.ShapeDtypeStruct((total, panel_shape[2]), jnp.bfloat16)
    away, keep, *all_arrays = pl.pallas_call(
        kernel,
        out_shape=[
            jax.ShapeDtypeStruct(shape, jnp.bfloat16),
            jax.ShapeDtypeStruct(shape, jnp.float32),
            kept_shape,
            kept_shape,
        ],
        in_specs=specs,
        out_specs=[VMEM, VMEM, HBM, HBM],
        scratch_shapes=[
            pltpu.VMEM(panel_shape, jnp.bfloat16),
            pltpu.SemaphoreType.DMA((2,)),
            *[pltpu.VMEM(slot, jnp.bfloat16) for slot in slots],
            *[pltpu.SemaphoreType.DMA((2, slot[0])) for slot in slots[:1]],
        ],
        input_output_aliases=aliases,
        compiler_params=pltpu.CompilerParams(vmem_limit_bytes=STREAM_LIMIT if slots else LIMIT),
        cost_estimate=pl.CostEstimate(flops=COST, bytes_accessed=0, transcendentals=0),
    )(*inputs)
    return away, keep, all_arrays


def in_terms(at, blocks, weights, kept_arrays, first, n, total):
    width, ff = weights[0].shape
    stream = kept_arrays is None
    return terms_call(
        functools.partial(in_kernel, first, stream),
        at,
        blocks,
        weights,
        kept_arrays,
        total,
        (2, 2 * n, ff),
        (2, 4 * n, width),
        [(3, width, 512), (3, 512, width)] if stream else (),
    )


def out_terms(at, own, got, weights, kept_arrays, first, total):
    width, ff = weights[0].shape
    n = own.shape[1]
    return terms_call(
        functools.partial(out_kernel, first),
        at,
        (own, got),
        weights,
        kept_arrays,
        total,
        (2, 2 * n, width // 2),
        (2, 2 * n, ff),
    )


class Clock:
    def __init__(self):
        self.last = None

    def start(self, value):
        if self.last is None:
            return value
        return lax.optimization_barrier((value, self.last))[0]

    def end(self, value):
        self.last = value
        return value


class Grid:
    def __init__(self, rows, cols, clock):
        self.rows, self.cols, self.clock = rows, cols, clock
        self.core = lax.axis_index("row") % 2
        self.at = jnp.reshape(lax.axis_index("col") % 2, (1,)).astype(jnp.int32)

    def gather(self, block):
        clock = self.clock
        block = transposed(clock.end(clock.start(block)), self.rows, self.cols)
        yield
        block = clock.end(clock.start(block))
        far = swap(block, "col", self.cols, 4)
        yield
        near = clock.end(jnp.concatenate([block, clock.start(far)], axis=1))
        far = swap(near, "col", self.cols, 2)
        yield
        far = clock.start(far)
        mine = jnp.where(
            self.core == 0,
            jnp.concatenate([near, far], axis=1),
            jnp.concatenate([far, near], axis=1),
        )
        mine = clock.end(mine)
        other = swap(mine, "col", self.cols, 1)
        yield
        return mine, clock.start(other)

    def scatter(self, away, keep):
        clock, n = self.clock, keep.shape[1] // 4
        clock.end(away)
        got = swap(away, "col", self.cols, 1)
        yield
        total = keep + clock.start(got)
        away = lax.dynamic_slice_in_dim(total, (1 - self.core) * 2 * n, 2 * n, axis=1)
        away = clock.end(away.astype(jnp.bfloat16))
        keep = lax.dynamic_slice_in_dim(total, self.core * 2 * n, 2 * n, axis=1)
        got = swap(away, "col", self.cols, 2)
        yield
        total = keep + clock.start(got)
        away = clock.end(total[:, n:].astype(jnp.bfloat16))
        got = swap(away, "col", self.cols, 4)
        yield
        out = clock.end((total[:, :n] + clock.start(got)).astype(jnp.bfloat16))
        out = transposed(out, self.rows, self.cols)
        yield
        return clock.end(clock.start(out))


def part_steps(grid, block, weights, kept_arrays, first, total):
    clock, rows, n = grid.clock, grid.rows, block.shape[1]
    blocks = yield from grid.gather(block)
    away, keep, kept_arrays["tokens"] = in_terms(
        grid.at, blocks, weights, kept_arrays.get("tokens"), first, n, total
    )
    got = swap(clock.end(away), "row", rows, 1)
    yield
    sums = keep + clock.start(got)
    got = swap(clock.end(sums.astype(jnp.bfloat16)), "row", rows, 2)
    yield
    act, grad_pre = activations(sums + clock.start(got))
    own = clock.end(jnp.stack([act, grad_pre]))
    got = swap(own, "row", rows, 1)
    yield
    away, keep, kept_arrays["hidden"] = out_terms(
        grid.at, own, clock.start(got), weights, kept_arrays.get("hidden"), first, total
    )
    return (yield from grid.scatter(away, keep))


def body(rows, cols, tokens, weight_in, weight_out, out_grad):
    clock = Clock()
    grid = Grid(rows, cols, clock)
    both = jnp.stack([tokens, out_grad])
    count = tokens.shape[0]
    size = [count * share // sum(SHARES) for share in SHARES]
    outs, kept_arrays = [None] * len(size), {}

    def run(part):
        first = sum(size[:part])
        outs[part] = yield from part_steps(
            grid,
            both[:, first : first + size[part]],
            (weight_in, weight_out),
            kept_arrays,
            rows * first,
            rows * count,
        )

    parts = [run(part) for part in range(len(size))]
    grads = []
    for part in ORDER:
        if part >= 0:
            next(parts[part], None)
            continue
        panel, full = kept_arrays["tokens"][len(grads)], kept_arrays["hidden"][1 - len(grads)]
        full = clock.start(full)
        grad = contract(full, panel, 0, 0) if grads else contract(panel, full, 0, 0)
        grads.append(clock.end(grad.astype(jnp.bfloat16)))
    out = jnp.concatenate(outs, axis=1)
    return out[0], out[1], grads[0], grads[1]


def plain_body(rows, cols, tokens, weight_in, weight_out, out_grad):
    per = cols // rows
    both = jnp.stack([tokens, out_grad])
    two, n, f = both.shape
    panel = lax.all_gather(transposed(both, rows, cols), "col", axis=0)
    panel = panel.reshape(rows, per, two, n, f).transpose(2, 0, 3, 1, 4).reshape(two, rows * n, per * f)
    terms = jnp.stack([contract(panel[0], weight_in, 1, 0), contract(panel[1], weight_out, 1, 1)])
    act, grad_pre = activations(lax.psum_scatter(terms, "row", scatter_dimension=1, tiled=True))
    full = lax.all_gather(jnp.stack([act, grad_pre]), "row", axis=1, tiled=True)
    terms = jnp.stack([contract(full[0], weight_out, 1, 0), contract(full[1], weight_in, 1, 1)])
    terms = terms.reshape(two, rows, n, per, f).transpose(1, 3, 0, 2, 4).reshape(cols, two, n, f)
    out = lax.psum_scatter(terms, "col", scatter_dimension=0).astype(jnp.bfloat16)
    out = transposed(out, rows, cols)
    grad_in = contract(panel[0], full[1], 0, 0).astype(jnp.bfloat16)
    grad_out = contract(full[0], panel[1], 0, 0).astype(jnp.bfloat16)
    return out[0], out[1], grad_in, grad_out


def solution(mesh):
    shape = (mesh.shape["row"], mesh.shape["col"])
    return jax.shard_map(
        functools.partial(body if shape == (4, 8) else plain_body, *shape),
        mesh=mesh,
        in_specs=(P("row", "col"), P("row", "col"), P("col", "row"), P("row", "col")),
        out_specs=(P("row", "col"), P("row", "col"), P("row", "col"), P("col", "row")),
        check_vma=False,
    )
```

```python
import functools

import jax
import jax.numpy as jnp
from jax import lax
from jax.experimental import pallas as pl
from jax.experimental.pallas import tpu as pltpu
from jax.sharding import PartitionSpec as P

LIMIT = 6 << 20
STREAM_LIMIT = 48 << 20
COST = 10**9

SHARES = (2, 2, 2, 2)
ORDER = (
    0, 0, 1, 0, 1, 0, 1, 2, 0, 1, 2, 0, 2, 3, 1, 0, 1, 2, 0, 3, 2, 3, 1, 2, 3, 1, 0, 3, 2, 3,
    0, 1, 2, 0, 1, 1, 0, 2, 3, 3, 1, 2, -1, 3, 2, 3, 2, 3, -1, 3,
)


VMEM = pl.BlockSpec(memory_space=pltpu.VMEM)
SMEM = pl.BlockSpec(memory_space=pltpu.SMEM)
HBM = pl.BlockSpec(memory_space=pltpu.HBM)


def cdf_of(value):
    return 0.5 * (1.0 + lax.erf(value * 0.7071067811865476))


def contract(left, right, left_dim, right_dim):
    return lax.dot_general(
        left, right, (((left_dim,), (right_dim,)), ((), ())), preferred_element_type=jnp.float32
    )


def activations(sums):
    hidden_pre, grad_act = sums[0], sums[1]
    cumul = cdf_of(hidden_pre)
    density = jnp.exp(-0.5 * hidden_pre * hidden_pre) * 0.3989422804014327
    act = (hidden_pre * cumul).astype(jnp.bfloat16)
    return act, (grad_act * (cumul + hidden_pre * density)).astype(jnp.bfloat16)


def swap(value, axis, size, mask):
    return lax.ppermute(value, axis, [(i, i ^ mask) for i in range(size)])


def transposed(value, rows, cols):
    per = cols // rows
    pairs = [
        (r * cols + c, (c // per) * cols + r * per + c % per) for r in range(rows) for c in range(cols)
    ]
    return lax.ppermute(value, ("row", "col"), pairs)


def streamed(sources, slots, sems, count, use):
    depth = slots[0].shape[0]

    def copies(j):
        return [
            pltpu.make_async_copy(source(j), slot.at[j % depth], sems.at[i, j % depth])
            for i, (source, slot) in enumerate(zip(sources, slots))
        ]

    for j in range(min(depth - 1, count)):
        for copy in copies(j):
            copy.start()
    for j in range(count):
        if j + depth - 1 < count:
            for copy in copies(j + depth - 1):
                copy.start()
        for copy in copies(j):
            copy.wait()
        use(j, j % depth)


def kept(sems, *pairs):
    copies = [pltpu.make_async_copy(*pair, sems.at[i]) for i, pair in enumerate(pairs)]
    for copy in copies:
        copy.start()
    return copies


def in_kernel(first, stream, at_ref, mine, other, weight_in, weight_out, *refs):
    away, keep, tok_all, grad_all, panel, keep_sems, *streaming = refs[-9:] if stream else refs[-6:]
    half, f = keep.shape[1], panel.shape[2] // 2
    side = at_ref[0]
    panel[:, :, pl.ds(pl.multiple_of(side * f, f), f)] = mine[...]
    panel[:, :, pl.ds(pl.multiple_of((1 - side) * f, f), f)] = other[...]
    rows = pl.ds(first, 2 * half)
    copies = kept(keep_sems, (panel.at[0], tok_all.at[rows]), (panel.at[1], grad_all.at[rows]))
    tile = 512

    def use(j, in_tile, out_tile):
        cols = slice(j * tile, (j + 1) * tile)
        hidden = contract(panel[0], in_tile, 1, 0)
        keep[0, :, cols] = hidden[:half]
        away[0, :, cols] = hidden[half:].astype(away.dtype)
        grad = contract(panel[1], out_tile, 1, 1)
        keep[1, :, cols] = grad[:half]
        away[1, :, cols] = grad[half:].astype(away.dtype)

    count = weight_in.shape[1] // tile
    if stream:
        in_slots, out_slots, sems = streaming
        streamed(
            [lambda j: weight_in.at[:, pl.ds(j * tile, tile)], lambda j: weight_out.at[pl.ds(j * tile, tile)]],
            [in_slots, out_slots],
            sems,
            count,
            lambda j, slot: use(j, in_slots[slot], out_slots[slot]),
        )
    else:
        for j in range(count):
            cols = slice(j * tile, (j + 1) * tile)
            use(j, weight_in[:, cols], weight_out[cols])
    for copy in copies:
        copy.wait()


def out_kernel(first, at_ref, own, got, weight_in, weight_out, *refs):
    away, keep, act_all, pre_all, full, keep_sems = refs[-6:]
    half, f = own.shape[1], keep.shape[2]
    full[:, :half] = own[...]
    full[:, half:] = got[...]
    rows = pl.ds(first, 2 * half)
    copies = kept(keep_sems, (full.at[0], act_all.at[rows]), (full.at[1], pre_all.at[rows]))
    tile = 256
    for out, side in ((away, 1 - at_ref[0]), (keep, at_ref[0])):
        for j in range(f // tile):
            cols = slice(j * tile, (j + 1) * tile)
            at = pl.ds(pl.multiple_of(side * f + j * tile, tile), tile)
            out[0, :, cols] = contract(full[0], weight_out[:, at], 1, 0).astype(out.dtype)
            out[1, :, cols] = contract(full[1], weight_in[at, :], 1, 1).astype(out.dtype)
    for copy in copies:
        copy.wait()


def terms_call(kernel, at, blocks, weights, all_arrays, total, shape, panel_shape, slots=()):
    inputs = [at, *blocks, *weights]
    specs = [SMEM] + [VMEM] * len(blocks) + [HBM if slots else VMEM] * len(weights)
    aliases = {}
    if all_arrays is not None:
        aliases = {len(inputs): 2, len(inputs) + 1: 3}
        inputs += all_arrays
        specs += [HBM] * 2
    kept_shape = jax.ShapeDtypeStruct((total, panel_shape[2]), jnp.bfloat16)
    away, keep, *all_arrays = pl.pallas_call(
        kernel,
        out_shape=[
            jax.ShapeDtypeStruct(shape, jnp.bfloat16),
            jax.ShapeDtypeStruct(shape, jnp.float32),
            kept_shape,
            kept_shape,
        ],
        in_specs=specs,
        out_specs=[VMEM, VMEM, HBM, HBM],
        scratch_shapes=[
            pltpu.VMEM(panel_shape, jnp.bfloat16),
            pltpu.SemaphoreType.DMA((2,)),
            *[pltpu.VMEM(slot, jnp.bfloat16) for slot in slots],
            *[pltpu.SemaphoreType.DMA((2, slot[0])) for slot in slots[:1]],
        ],
        input_output_aliases=aliases,
        compiler_params=pltpu.CompilerParams(vmem_limit_bytes=STREAM_LIMIT if slots else LIMIT),
        cost_estimate=pl.CostEstimate(flops=COST, bytes_accessed=0, transcendentals=0),
    )(*inputs)
    return away, keep, all_arrays


def in_terms(at, blocks, weights, kept_arrays, first, n, total):
    width, ff = weights[0].shape
    stream = kept_arrays is None
    return terms_call(
        functools.partial(in_kernel, first, stream),
        at,
        blocks,
        weights,
        kept_arrays,
        total,
        (2, 2 * n, ff),
        (2, 4 * n, width),
        [(3, width, 512), (3, 512, width)] if stream else (),
    )


def out_terms(at, own, got, weights, kept_arrays, first, total):
    width, ff = weights[0].shape
    n = own.shape[1]
    return terms_call(
        functools.partial(out_kernel, first),
        at,
        (own, got),
        weights,
        kept_arrays,
        total,
        (2, 2 * n, width // 2),
        (2, 2 * n, ff),
    )


class Clock:
    def __init__(self):
        self.last = None

    def start(self, value):
        if self.last is None:
            return value
        return lax.optimization_barrier((value, self.last))[0]

    def end(self, value):
        self.last = value
        return value


class Grid:
    def __init__(self, rows, cols, clock):
        self.rows, self.cols, self.clock = rows, cols, clock
        self.core = lax.axis_index("row") % 2
        self.at = jnp.reshape(lax.axis_index("col") % 2, (1,)).astype(jnp.int32)

    def gather(self, block):
        clock = self.clock
        block = transposed(clock.end(clock.start(block)), self.rows, self.cols)
        yield
        block = clock.end(clock.start(block))
        far = swap(block, "col", self.cols, 4)
        yield
        near = clock.end(jnp.concatenate([block, clock.start(far)], axis=1))
        far = swap(near, "col", self.cols, 2)
        yield
        far = clock.start(far)
        mine = jnp.where(
            self.core == 0,
            jnp.concatenate([near, far], axis=1),
            jnp.concatenate([far, near], axis=1),
        )
        mine = clock.end(mine)
        other = swap(mine, "col", self.cols, 1)
        yield
        return mine, clock.start(other)

    def scatter(self, away, keep):
        clock, n = self.clock, keep.shape[1] // 4
        clock.end(away)
        got = swap(away, "col", self.cols, 1)
        yield
        total = keep + clock.start(got)
        away = lax.dynamic_slice_in_dim(total, (1 - self.core) * 2 * n, 2 * n, axis=1)
        away = clock.end(away.astype(jnp.bfloat16))
        keep = lax.dynamic_slice_in_dim(total, self.core * 2 * n, 2 * n, axis=1)
        got = swap(away, "col", self.cols, 2)
        yield
        total = keep + clock.start(got)
        away = clock.end(total[:, n:].astype(jnp.bfloat16))
        got = swap(away, "col", self.cols, 4)
        yield
        out = clock.end((total[:, :n] + clock.start(got)).astype(jnp.bfloat16))
        out = transposed(out, self.rows, self.cols)
        yield
        return clock.end(clock.start(out))


def part_steps(grid, block, weights, kept_arrays, first, total):
    clock, rows, n = grid.clock, grid.rows, block.shape[1]
    blocks = yield from grid.gather(block)
    away, keep, kept_arrays["tokens"] = in_terms(
        grid.at, blocks, weights, kept_arrays.get("tokens"), first, n, total
    )
    got = swap(clock.end(away), "row", rows, 1)
    yield
    sums = keep + clock.start(got)
    got = swap(clock.end(sums.astype(jnp.bfloat16)), "row", rows, 2)
    yield
    act, grad_pre = activations(sums + clock.start(got))
    own = clock.end(jnp.stack([act, grad_pre]))
    got = swap(own, "row", rows, 1)
    yield
    away, keep, kept_arrays["hidden"] = out_terms(
        grid.at, own, clock.start(got), weights, kept_arrays.get("hidden"), first, total
    )
    return (yield from grid.scatter(away, keep))


def body(rows, cols, tokens, weight_in, weight_out, out_grad):
    clock = Clock()
    grid = Grid(rows, cols, clock)
    both = jnp.stack([tokens, out_grad])
    count = tokens.shape[0]
    size = [count * share // sum(SHARES) for share in SHARES]
    outs, kept_arrays = [None] * len(size), {}

    def run(part):
        first = sum(size[:part])
        outs[part] = yield from part_steps(
            grid,
            both[:, first : first + size[part]],
            (weight_in, weight_out),
            kept_arrays,
            rows * first,
            rows * count,
        )

    parts = [run(part) for part in range(len(size))]
    grads = []
    for part in ORDER:
        if part >= 0:
            next(parts[part], None)
            continue
        panel, full = kept_arrays["tokens"][len(grads)], kept_arrays["hidden"][1 - len(grads)]
        full = clock.start(full)
        grad = contract(full, panel, 0, 0) if grads else contract(panel, full, 0, 0)
        grads.append(clock.end(grad.astype(jnp.bfloat16)))
    out = jnp.concatenate(outs, axis=1)
    return out[0], out[1], grads[0], grads[1]


def plain_body(rows, cols, tokens, weight_in, weight_out, out_grad):
    per = cols // rows
    both = jnp.stack([tokens, out_grad])
    two, n, f = both.shape
    panel = lax.all_gather(transposed(both, rows, cols), "col", axis=0)
    panel = panel.reshape(rows, per, two, n, f).transpose(2, 0, 3, 1, 4).reshape(two, rows * n, per * f)
    terms = jnp.stack([contract(panel[0], weight_in, 1, 0), contract(panel[1], weight_out, 1, 1)])
    act, grad_pre = activations(lax.psum_scatter(terms, "row", scatter_dimension=1, tiled=True))
    full = lax.all_gather(jnp.stack([act, grad_pre]), "row", axis=1, tiled=True)
    terms = jnp.stack([contract(full[0], weight_out, 1, 0), contract(full[1], weight_in, 1, 1)])
    terms = terms.reshape(two, rows, n, per, f).transpose(1, 3, 0, 2, 4).reshape(cols, two, n, f)
    out = lax.psum_scatter(terms, "col", scatter_dimension=0).astype(jnp.bfloat16)
    out = transposed(out, rows, cols)
    grad_in = contract(panel[0], full[1], 0, 0).astype(jnp.bfloat16)
    grad_out = contract(full[0], panel[1], 0, 0).astype(jnp.bfloat16)
    return out[0], out[1], grad_in, grad_out


def solution(mesh):
    shape = (mesh.shape["row"], mesh.shape["col"])
    return jax.shard_map(
        functools.partial(body if shape == (4, 8) else plain_body, *shape),
        mesh=mesh,
        in_specs=(P("row", "col"), P("row", "col"), P("col", "row"), P("row", "col")),
        out_specs=(P("row", "col"), P("row", "col"), P("row", "col"), P("col", "row")),
        check_vma=False,
    )
```

```python
import functools

import jax
import jax.numpy as jnp
from jax import lax
from jax.experimental import pallas as pl
from jax.experimental.pallas import tpu as pltpu
from jax.sharding import PartitionSpec as P

LIMIT = 6 << 20
STREAM_LIMIT = 48 << 20
COST = 10**9

SHARES = (2, 2, 2, 2)
ORDER = (
    0, 0, 1, 0, 1, 0, 1, 2, 0, 1, 2, 0, 2, 3, 1, 0, 1, 2, 0, 3, 2, 3, 1, 2, 3, 1, 0, 3, 2, 3,
    0, 1, 2, 0, 1, 1, 0, 2, 3, -2, 3, -2, 1, 2, -1, 3, 2, 3, 2, 3, -1, 3,
)


VMEM = pl.BlockSpec(memory_space=pltpu.VMEM)
SMEM = pl.BlockSpec(memory_space=pltpu.SMEM)
HBM = pl.BlockSpec(memory_space=pltpu.HBM)


def cdf_of(value):
    return 0.5 * (1.0 + lax.erf(value * 0.7071067811865476))


def contract(left, right, left_dim, right_dim):
    return lax.dot_general(
        left, right, (((left_dim,), (right_dim,)), ((), ())), preferred_element_type=jnp.float32
    )


def activations(sums):
    hidden_pre, grad_act = sums[0], sums[1]
    cumul = cdf_of(hidden_pre)
    density = jnp.exp(-0.5 * hidden_pre * hidden_pre) * 0.3989422804014327
    act = (hidden_pre * cumul).astype(jnp.bfloat16)
    return act, (grad_act * (cumul + hidden_pre * density)).astype(jnp.bfloat16)


def swap(value, axis, size, mask):
    return lax.ppermute(value, axis, [(i, i ^ mask) for i in range(size)])


def transposed(value, rows, cols):
    per = cols // rows
    pairs = [
        (r * cols + c, (c // per) * cols + r * per + c % per) for r in range(rows) for c in range(cols)
    ]
    return lax.ppermute(value, ("row", "col"), pairs)


def streamed(sources, slots, sems, count, use):
    depth = slots[0].shape[0]

    def copies(j):
        return [
            pltpu.make_async_copy(source(j), slot.at[j % depth], sems.at[i, j % depth])
            for i, (source, slot) in enumerate(zip(sources, slots))
        ]

    for j in range(min(depth - 1, count)):
        for copy in copies(j):
            copy.start()
    for j in range(count):
        if j + depth - 1 < count:
            for copy in copies(j + depth - 1):
                copy.start()
        for copy in copies(j):
            copy.wait()
        use(j, j % depth)


def store_kernel(firsts, at_ref, *refs):
    arrays, sems = refs[-5:-1], refs[-1]
    copies = []
    for i, first in enumerate(firsts):
        mine, other, own, got = refs[4 * i : 4 * i + 4]
        n, f = mine.shape[1], mine.shape[2]
        for k in range(2):
            for block, side in ((mine, at_ref[0]), (other, 1 - at_ref[0])):
                cols = pl.ds(pl.multiple_of(side * f, f), f)
                copies.append((block.at[k], arrays[k].at[pl.ds(first, n), cols]))
            for block, at in ((own, first), (got, first + n // 2)):
                copies.append((block.at[k], arrays[2 + k].at[pl.ds(at, n // 2)]))
    copies = [pltpu.make_async_copy(*pair, sems.at[i]) for i, pair in enumerate(copies)]
    for copy in copies:
        copy.start()
    for copy in copies:
        copy.wait()


def stored(at, firsts, pieces, arrays, total):
    mine, _, own, _ = pieces[0]
    shapes = [jax.ShapeDtypeStruct((total, width), jnp.bfloat16) for width in [2 * mine.shape[2]] * 2 + [own.shape[2]] * 2]
    inputs = [piece for part in pieces for piece in part]
    aliases = {1 + len(inputs) + i: i for i in range(4)} if arrays else {}
    return pl.pallas_call(
        functools.partial(store_kernel, firsts),
        out_shape=shapes,
        in_specs=[SMEM] + [pl.BlockSpec(memory_space=pl.ANY)] * len(inputs) + [VMEM] * len(aliases),
        out_specs=[VMEM] * 4,
        scratch_shapes=[pltpu.SemaphoreType.DMA((2 * len(inputs),))],
        input_output_aliases=aliases,
        compiler_params=pltpu.CompilerParams(vmem_limit_bytes=LIMIT),
        cost_estimate=pl.CostEstimate(flops=COST, bytes_accessed=0, transcendentals=0),
    )(at, *inputs, *(arrays or ()))


def in_kernel(stream, at_ref, mine, other, weight_in, weight_out, *refs):
    away, keep, panel, *streaming = refs
    half, f = keep.shape[1], panel.shape[2] // 2
    side = at_ref[0]
    panel[:, :, pl.ds(pl.multiple_of(side * f, f), f)] = mine[...]
    panel[:, :, pl.ds(pl.multiple_of((1 - side) * f, f), f)] = other[...]
    tile = 512

    def use(j, in_tile, out_tile):
        cols = slice(j * tile, (j + 1) * tile)
        hidden = contract(panel[0], in_tile, 1, 0)
        keep[0, :, cols] = hidden[:half]
        away[0, :, cols] = hidden[half:].astype(away.dtype)
        grad = contract(panel[1], out_tile, 1, 1)
        keep[1, :, cols] = grad[:half]
        away[1, :, cols] = grad[half:].astype(away.dtype)

    count = weight_in.shape[1] // tile
    if stream:
        in_slots, out_slots, sems = streaming
        streamed(
            [lambda j: weight_in.at[:, pl.ds(j * tile, tile)], lambda j: weight_out.at[pl.ds(j * tile, tile)]],
            [in_slots, out_slots],
            sems,
            count,
            lambda j, slot: use(j, in_slots[slot], out_slots[slot]),
        )
    else:
        for j in range(count):
            cols = slice(j * tile, (j + 1) * tile)
            use(j, weight_in[:, cols], weight_out[cols])


def out_kernel(at_ref, own, got, weight_in, weight_out, away, keep, full):
    half, f = own.shape[1], keep.shape[2]
    full[:, :half] = own[...]
    full[:, half:] = got[...]
    tile = 256
    for out, side in ((away, 1 - at_ref[0]), (keep, at_ref[0])):
        for j in range(f // tile):
            cols = slice(j * tile, (j + 1) * tile)
            at = pl.ds(pl.multiple_of(side * f + j * tile, tile), tile)
            out[0, :, cols] = contract(full[0], weight_out[:, at], 1, 0).astype(out.dtype)
            out[1, :, cols] = contract(full[1], weight_in[at, :], 1, 1).astype(out.dtype)


def terms_call(kernel, at, blocks, weights, shape, panel_shape, slots=()):
    return pl.pallas_call(
        kernel,
        out_shape=[jax.ShapeDtypeStruct(shape, jnp.bfloat16), jax.ShapeDtypeStruct(shape, jnp.float32)],
        in_specs=[SMEM] + [VMEM] * len(blocks) + [HBM if slots else VMEM] * len(weights),
        out_specs=[VMEM, VMEM],
        scratch_shapes=[
            pltpu.VMEM(panel_shape, jnp.bfloat16),
            *[pltpu.VMEM(slot, jnp.bfloat16) for slot in slots],
            *[pltpu.SemaphoreType.DMA((2, slot[0])) for slot in slots[:1]],
        ],
        compiler_params=pltpu.CompilerParams(vmem_limit_bytes=STREAM_LIMIT if slots else LIMIT),
        cost_estimate=pl.CostEstimate(flops=COST, bytes_accessed=0, transcendentals=0),
    )(at, *blocks, *weights)


def in_terms(at, blocks, weights, stream):
    width, ff = weights[0].shape
    n = blocks[0].shape[1]
    return terms_call(
        functools.partial(in_kernel, stream),
        at,
        blocks,
        weights,
        (2, n // 2, ff),
        (2, n, width),
        [(3, width, 512), (3, 512, width)] if stream else (),
    )


def out_terms(at, own, got, weights):
    width, ff = weights[0].shape
    n = 2 * own.shape[1]
    return terms_call(out_kernel, at, (own, got), weights, (2, n, width // 2), (2, n, ff))


class Clock:
    def __init__(self):
        self.last = None

    def start(self, value):
        if self.last is None:
            return value
        return lax.optimization_barrier((value, self.last))[0]

    def end(self, value):
        self.last = value
        return value


class Grid:
    def __init__(self, rows, cols, clock):
        self.rows, self.cols, self.clock = rows, cols, clock
        self.core = lax.axis_index("row") % 2
        self.at = jnp.reshape(lax.axis_index("col") % 2, (1,)).astype(jnp.int32)

    def gather(self, block):
        clock = self.clock
        block = transposed(clock.end(clock.start(block)), self.rows, self.cols)
        yield
        block = clock.end(clock.start(block))
        far = swap(block, "col", self.cols, 4)
        yield
        near = clock.end(jnp.concatenate([block, clock.start(far)], axis=1))
        far = swap(near, "col", self.cols, 2)
        yield
        far = clock.start(far)
        mine = jnp.where(
            self.core == 0,
            jnp.concatenate([near, far], axis=1),
            jnp.concatenate([far, near], axis=1),
        )
        mine = clock.end(mine)
        other = swap(mine, "col", self.cols, 1)
        yield
        return mine, clock.start(other)

    def scatter(self, away, keep):
        clock, n = self.clock, keep.shape[1] // 4
        clock.end(away)
        got = swap(away, "col", self.cols, 1)
        yield
        total = keep + clock.start(got)
        away = lax.dynamic_slice_in_dim(total, (1 - self.core) * 2 * n, 2 * n, axis=1)
        away = clock.end(away.astype(jnp.bfloat16))
        keep = lax.dynamic_slice_in_dim(total, self.core * 2 * n, 2 * n, axis=1)
        got = swap(away, "col", self.cols, 2)
        yield
        total = keep + clock.start(got)
        away = clock.end(total[:, n:].astype(jnp.bfloat16))
        got = swap(away, "col", self.cols, 4)
        yield
        out = clock.end((total[:, :n] + clock.start(got)).astype(jnp.bfloat16))
        out = transposed(out, self.rows, self.cols)
        yield
        return clock.end(clock.start(out))


def part_steps(grid, block, weights, stream, made):
    clock, rows = grid.clock, grid.rows
    blocks = yield from grid.gather(block)
    away, keep = in_terms(grid.at, blocks, weights, stream)
    got = swap(clock.end(away), "row", rows, 1)
    yield
    sums = keep + clock.start(got)
    got = swap(clock.end(sums.astype(jnp.bfloat16)), "row", rows, 2)
    yield
    act, grad_pre = activations(sums + clock.start(got))
    own = clock.end(jnp.stack([act, grad_pre]))
    got = swap(own, "row", rows, 1)
    yield
    got = clock.start(got)
    made["pieces"] = *blocks, own, got
    made["out"] = yield from grid.scatter(*out_terms(grid.at, own, got, weights))


def body(rows, cols, tokens, weight_in, weight_out, out_grad):
    clock = Clock()
    grid = Grid(rows, cols, clock)
    both = jnp.stack([tokens, out_grad])
    count = tokens.shape[0]
    size = [count * share // sum(SHARES) for share in SHARES]
    start = [sum(size[:part]) for part in range(len(size))]
    made = [{} for _ in size]
    parts = [
        part_steps(grid, both[:, at : at + n], (weight_in, weight_out), not at, out)
        for at, n, out in zip(start, size, made)
    ]
    arrays, grads = (), []
    stores = [list(range(len(size) - 1)), [len(size) - 1]]
    for part in ORDER:
        if part == -2:
            now = stores.pop(0)
            pieces = [made[i]["pieces"] for i in now]
            pieces[0] = (clock.start(pieces[0][0]), *pieces[0][1:])
            arrays = stored(grid.at, [rows * start[i] for i in now], pieces, arrays, rows * count)
            clock.end(arrays[3])
        elif part == -1:
            panel, full = arrays[len(grads)], clock.start(arrays[3 - len(grads)])
            grad = contract(full, panel, 0, 0) if grads else contract(panel, full, 0, 0)
            grads.append(clock.end(grad.astype(jnp.bfloat16)))
        else:
            next(parts[part], None)
    out = jnp.concatenate([m["out"] for m in made], axis=1)
    return out[0], out[1], grads[0], grads[1]


def plain_body(rows, cols, tokens, weight_in, weight_out, out_grad):
    per = cols // rows
    both = jnp.stack([tokens, out_grad])
    two, n, f = both.shape
    panel = lax.all_gather(transposed(both, rows, cols), "col", axis=0)
    panel = panel.reshape(rows, per, two, n, f).transpose(2, 0, 3, 1, 4).reshape(two, rows * n, per * f)
    terms = jnp.stack([contract(panel[0], weight_in, 1, 0), contract(panel[1], weight_out, 1, 1)])
    act, grad_pre = activations(lax.psum_scatter(terms, "row", scatter_dimension=1, tiled=True))
    full = lax.all_gather(jnp.stack([act, grad_pre]), "row", axis=1, tiled=True)
    terms = jnp.stack([contract(full[0], weight_out, 1, 0), contract(full[1], weight_in, 1, 1)])
    terms = terms.reshape(two, rows, n, per, f).transpose(1, 3, 0, 2, 4).reshape(cols, two, n, f)
    out = lax.psum_scatter(terms, "col", scatter_dimension=0).astype(jnp.bfloat16)
    out = transposed(out, rows, cols)
    grad_in = contract(panel[0], full[1], 0, 0).astype(jnp.bfloat16)
    grad_out = contract(full[0], panel[1], 0, 0).astype(jnp.bfloat16)
    return out[0], out[1], grad_in, grad_out


def solution(mesh):
    shape = (mesh.shape["row"], mesh.shape["col"])
    return jax.shard_map(
        functools.partial(body if shape == (4, 8) else plain_body, *shape),
        mesh=mesh,
        in_specs=(P("row", "col"), P("row", "col"), P("col", "row"), P("row", "col")),
        out_specs=(P("row", "col"), P("row", "col"), P("row", "col"), P("col", "row")),
        check_vma=False,
    )
```

```python
import functools

import jax
import jax.numpy as jnp
from jax import lax
from jax.experimental import pallas as pl
from jax.experimental.pallas import tpu as pltpu
from jax.sharding import PartitionSpec as P

LIMIT = 4 << 20
STREAM_LIMIT = 48 << 20
COST = 10**9

SHARES = (2, 2, 2, 2)
ORDER = (
    0, 0, 0, 1, 0, 1, 0, 1, 2, 0, 1, 2, 2, 3, 1, 0, 1, 2, 3, 0, 3, 2, 3, 1, 2, 1, 0, 3, 2, 3,
    0, 1, 2, 0, 1, 1, 0, 2, 3, -2, 3, -2, 1, 2, -1, 3, 2, 3, 2, 3, -1, 3,
)


VMEM = pl.BlockSpec(memory_space=pltpu.VMEM)
SMEM = pl.BlockSpec(memory_space=pltpu.SMEM)
HBM = pl.BlockSpec(memory_space=pltpu.HBM)


def cdf_of(value):
    return 0.5 * (1.0 + lax.erf(value * 0.7071067811865476))


def contract(left, right, left_dim, right_dim):
    return lax.dot_general(
        left, right, (((left_dim,), (right_dim,)), ((), ())), preferred_element_type=jnp.float32
    )


def activations(sums):
    hidden_pre, grad_act = sums[0], sums[1]
    cumul = cdf_of(hidden_pre)
    density = jnp.exp(-0.5 * hidden_pre * hidden_pre) * 0.3989422804014327
    act = (hidden_pre * cumul).astype(jnp.bfloat16)
    return act, (grad_act * (cumul + hidden_pre * density)).astype(jnp.bfloat16)


def swap(value, axis, size, mask):
    return lax.ppermute(value, axis, [(i, i ^ mask) for i in range(size)])


def transposed(value, rows, cols):
    per = cols // rows
    pairs = [
        (r * cols + c, (c // per) * cols + r * per + c % per) for r in range(rows) for c in range(cols)
    ]
    return lax.ppermute(value, ("row", "col"), pairs)


def streamed(sources, slots, sems, count, use):
    depth = slots[0].shape[0]

    def copies(j):
        return [
            pltpu.make_async_copy(source(j), slot.at[j % depth], sems.at[i, j % depth])
            for i, (source, slot) in enumerate(zip(sources, slots))
        ]

    for j in range(min(depth - 1, count)):
        for copy in copies(j):
            copy.start()
    for j in range(count):
        if j + depth - 1 < count:
            for copy in copies(j + depth - 1):
                copy.start()
        for copy in copies(j):
            copy.wait()
        use(j, j % depth)


def store_kernel(firsts, hidden, at_ref, *refs):
    arrays, sems = refs[-3:-1], refs[-1]
    copies = []
    for i, first in enumerate(firsts):
        for j, block in enumerate(refs[2 * i : 2 * i + 2]):
            n, f = block.shape[1:]
            side = at_ref[0] if j == 0 else 1 - at_ref[0]
            for k in range(2):
                if hidden:
                    rows = arrays[k].at[pl.ds(first + j * n, n)]
                else:
                    rows = arrays[k].at[pl.ds(first, n), pl.ds(pl.multiple_of(side * f, f), f)]
                copies.append((block.at[k], rows))
    copies = [pltpu.make_async_copy(*pair, sems.at[i]) for i, pair in enumerate(copies)]
    for copy in copies:
        copy.start()
    for copy in copies:
        copy.wait()


def stored(at, firsts, pieces, hidden, total):
    inputs = [piece for part in pieces for piece in part]
    width = inputs[0].shape[2] * (1 if hidden else 2)
    return pl.pallas_call(
        functools.partial(store_kernel, firsts, hidden),
        out_shape=[jax.ShapeDtypeStruct((total, width), jnp.bfloat16)] * 2,
        in_specs=[SMEM] + [pl.BlockSpec(memory_space=pl.ANY)] * len(inputs),
        out_specs=[VMEM] * 2,
        scratch_shapes=[pltpu.SemaphoreType.DMA((2 * len(inputs),))],
        compiler_params=pltpu.CompilerParams(vmem_limit_bytes=LIMIT),
        cost_estimate=pl.CostEstimate(flops=COST, bytes_accessed=0, transcendentals=0),
    )(at, *inputs)


def in_kernel(stream, at_ref, mine, other, weight_in, weight_out, *refs):
    away, keep, panel, *streaming = refs
    half, f = keep.shape[1], panel.shape[2] // 2
    side = at_ref[0]
    panel[:, :, pl.ds(pl.multiple_of(side * f, f), f)] = mine[...]
    panel[:, :, pl.ds(pl.multiple_of((1 - side) * f, f), f)] = other[...]
    tile = 512

    def use(j, in_tile, out_tile):
        cols = slice(j * tile, (j + 1) * tile)
        hidden = contract(panel[0], in_tile, 1, 0)
        keep[0, :, cols] = hidden[:half]
        away[0, :, cols] = hidden[half:].astype(away.dtype)
        grad = contract(panel[1], out_tile, 1, 1)
        keep[1, :, cols] = grad[:half]
        away[1, :, cols] = grad[half:].astype(away.dtype)

    count = weight_in.shape[1] // tile
    if stream:
        in_slots, out_slots, sems = streaming
        streamed(
            [lambda j: weight_in.at[:, pl.ds(j * tile, tile)], lambda j: weight_out.at[pl.ds(j * tile, tile)]],
            [in_slots, out_slots],
            sems,
            count,
            lambda j, slot: use(j, in_slots[slot], out_slots[slot]),
        )
    else:
        for j in range(count):
            cols = slice(j * tile, (j + 1) * tile)
            use(j, weight_in[:, cols], weight_out[cols])


def out_kernel(at_ref, own, got, weight_in, weight_out, away, keep, full):
    half, f = own.shape[1], keep.shape[2]
    full[:, :half] = own[...]
    full[:, half:] = got[...]
    tile = 256
    for out, side in ((away, 1 - at_ref[0]), (keep, at_ref[0])):
        for j in range(f // tile):
            cols = slice(j * tile, (j + 1) * tile)
            at = pl.ds(pl.multiple_of(side * f + j * tile, tile), tile)
            out[0, :, cols] = contract(full[0], weight_out[:, at], 1, 0).astype(out.dtype)
            out[1, :, cols] = contract(full[1], weight_in[at, :], 1, 1).astype(out.dtype)


def terms_call(kernel, at, blocks, weights, shape, panel_shape, slots=()):
    return pl.pallas_call(
        kernel,
        out_shape=[jax.ShapeDtypeStruct(shape, jnp.bfloat16), jax.ShapeDtypeStruct(shape, jnp.float32)],
        in_specs=[SMEM] + [VMEM] * len(blocks) + [HBM if slots else VMEM] * len(weights),
        out_specs=[VMEM, VMEM],
        scratch_shapes=[
            pltpu.VMEM(panel_shape, jnp.bfloat16),
            *[pltpu.VMEM(slot, jnp.bfloat16) for slot in slots],
            *[pltpu.SemaphoreType.DMA((2, slot[0])) for slot in slots[:1]],
        ],
        compiler_params=pltpu.CompilerParams(vmem_limit_bytes=STREAM_LIMIT if slots else LIMIT),
        cost_estimate=pl.CostEstimate(flops=COST, bytes_accessed=0, transcendentals=0),
    )(at, *blocks, *weights)


def in_terms(at, blocks, weights, stream):
    width, ff = weights[0].shape
    n = blocks[0].shape[1]
    return terms_call(
        functools.partial(in_kernel, stream),
        at,
        blocks,
        weights,
        (2, n // 2, ff),
        (2, n, width),
        [(3, width, 512), (3, 512, width)] if stream else (),
    )


def out_terms(at, own, got, weights):
    width, ff = weights[0].shape
    n = 2 * own.shape[1]
    return terms_call(out_kernel, at, (own, got), weights, (2, n, width // 2), (2, n, ff))


class Clock:
    def __init__(self):
        self.last = None

    def start(self, value):
        if self.last is None:
            return value
        return lax.optimization_barrier((value, self.last))[0]

    def end(self, value):
        self.last = value
        return value


class Grid:
    def __init__(self, rows, cols, clock):
        self.rows, self.cols, self.clock = rows, cols, clock
        self.core = lax.axis_index("row") % 2
        self.at = jnp.reshape(lax.axis_index("col") % 2, (1,)).astype(jnp.int32)

    def gather(self, block):
        clock = self.clock
        block = transposed(clock.end(clock.start(block)), self.rows, self.cols)
        yield
        block = clock.end(clock.start(block))
        far = swap(block, "col", self.cols, 4)
        yield
        near = clock.end(jnp.concatenate([block, clock.start(far)], axis=1))
        far = swap(near, "col", self.cols, 2)
        yield
        far = clock.start(far)
        mine = jnp.where(
            self.core == 0,
            jnp.concatenate([near, far], axis=1),
            jnp.concatenate([far, near], axis=1),
        )
        mine = clock.end(mine)
        other = swap(mine, "col", self.cols, 1)
        yield
        return mine, clock.start(other)

    def scatter(self, away, keep):
        clock, n = self.clock, keep.shape[1] // 4
        clock.end(away)
        got = swap(away, "col", self.cols, 1)
        yield
        total = keep + clock.start(got)
        away = lax.dynamic_slice_in_dim(total, (1 - self.core) * 2 * n, 2 * n, axis=1)
        away = clock.end(away.astype(jnp.bfloat16))
        keep = lax.dynamic_slice_in_dim(total, self.core * 2 * n, 2 * n, axis=1)
        got = swap(away, "col", self.cols, 2)
        yield
        total = keep + clock.start(got)
        away = clock.end(total[:, n:].astype(jnp.bfloat16))
        got = swap(away, "col", self.cols, 4)
        yield
        out = clock.end((total[:, :n] + clock.start(got)).astype(jnp.bfloat16))
        out = transposed(out, self.rows, self.cols)
        yield
        return clock.end(clock.start(out))


def part_steps(grid, block, weights, stream, made):
    clock, rows = grid.clock, grid.rows
    made["tokens"] = blocks = yield from grid.gather(block)
    away, keep = in_terms(grid.at, blocks, weights, stream)
    got = swap(clock.end(away), "row", rows, 1)
    yield
    sums = keep + clock.start(got)
    got = swap(clock.end(sums.astype(jnp.bfloat16)), "row", rows, 2)
    yield
    act, grad_pre = activations(sums + clock.start(got))
    own = clock.end(jnp.stack([act, grad_pre]))
    got = swap(own, "row", rows, 1)
    yield
    got = clock.start(got)
    made["hidden"] = own, got
    made["out"] = yield from grid.scatter(*out_terms(grid.at, own, got, weights))


def body(rows, cols, tokens, weight_in, weight_out, out_grad):
    clock = Clock()
    grid = Grid(rows, cols, clock)
    both = jnp.stack([tokens, out_grad])
    count = tokens.shape[0]
    size = [count * share // sum(SHARES) for share in SHARES]
    start = [sum(size[:part]) for part in range(len(size))]
    made = [{} for _ in size]
    parts = [
        part_steps(grid, both[:, at : at + n], (weight_in, weight_out), not at, out)
        for at, n, out in zip(start, size, made)
    ]
    arrays, grads = [], []
    for part in ORDER:
        if part == -2:
            pieces = [out["hidden" if arrays else "tokens"] for out in made]
            pieces[0] = (clock.start(pieces[0][0]), pieces[0][1])
            arrays += stored(grid.at, [rows * at for at in start], pieces, bool(arrays), rows * count)
            clock.end(arrays[-1])
        elif part == -1:
            panel, full = arrays[len(grads)], clock.start(arrays[3 - len(grads)])
            grad = contract(full, panel, 0, 0) if grads else contract(panel, full, 0, 0)
            grads.append(clock.end(grad.astype(jnp.bfloat16)))
        else:
            next(parts[part], None)
    out = jnp.concatenate([m["out"] for m in made], axis=1)
    return out[0], out[1], grads[0], grads[1]


def plain_body(rows, cols, tokens, weight_in, weight_out, out_grad):
    per = cols // rows
    both = jnp.stack([tokens, out_grad])
    two, n, f = both.shape
    panel = lax.all_gather(transposed(both, rows, cols), "col", axis=0)
    panel = panel.reshape(rows, per, two, n, f).transpose(2, 0, 3, 1, 4).reshape(two, rows * n, per * f)
    terms = jnp.stack([contract(panel[0], weight_in, 1, 0), contract(panel[1], weight_out, 1, 1)])
    act, grad_pre = activations(lax.psum_scatter(terms, "row", scatter_dimension=1, tiled=True))
    full = lax.all_gather(jnp.stack([act, grad_pre]), "row", axis=1, tiled=True)
    terms = jnp.stack([contract(full[0], weight_out, 1, 0), contract(full[1], weight_in, 1, 1)])
    terms = terms.reshape(two, rows, n, per, f).transpose(1, 3, 0, 2, 4).reshape(cols, two, n, f)
    out = lax.psum_scatter(terms, "col", scatter_dimension=0).astype(jnp.bfloat16)
    out = transposed(out, rows, cols)
    grad_in = contract(panel[0], full[1], 0, 0).astype(jnp.bfloat16)
    grad_out = contract(full[0], panel[1], 0, 0).astype(jnp.bfloat16)
    return out[0], out[1], grad_in, grad_out


def solution(mesh):
    shape = (mesh.shape["row"], mesh.shape["col"])
    return jax.shard_map(
        functools.partial(body if shape == (4, 8) else plain_body, *shape),
        mesh=mesh,
        in_specs=(P("row", "col"), P("row", "col"), P("col", "row"), P("row", "col")),
        out_specs=(P("row", "col"), P("row", "col"), P("row", "col"), P("col", "row")),
        check_vma=False,
    )
```

```python
import functools

import jax
import jax.numpy as jnp
from jax import lax
from jax.experimental import pallas as pl
from jax.experimental.pallas import tpu as pltpu
from jax.sharding import PartitionSpec as P

LIMIT = 6 << 20
STREAM_LIMIT = 48 << 20
COST = 10**9

SHARES = (2, 2, 2, 2)
ORDER = (
    0, 0, 1, 0, 1, 0, 1, 2, 0, 1, 2, 0, 2, 3, 1, 0, 1, 2, 0, 3, 2, 3, 1, 2, 3, 1, 0, 3, 2, 3,
    0, 1, 2, 0, 1, 1, 2, 3, -2, 3, -2, 0, 1, 2, -1, 3, 2, 3, 2, 3, -1, 3,
)


VMEM = pl.BlockSpec(memory_space=pltpu.VMEM)
SMEM = pl.BlockSpec(memory_space=pltpu.SMEM)
HBM = pl.BlockSpec(memory_space=pltpu.HBM)


def cdf_of(value):
    return 0.5 * (1.0 + lax.erf(value * 0.7071067811865476))


def contract(left, right, left_dim, right_dim):
    return lax.dot_general(
        left, right, (((left_dim,), (right_dim,)), ((), ())), preferred_element_type=jnp.float32
    )


def activations(sums):
    hidden_pre, grad_act = sums[0], sums[1]
    cumul = cdf_of(hidden_pre)
    density = jnp.exp(-0.5 * hidden_pre * hidden_pre) * 0.3989422804014327
    act = (hidden_pre * cumul).astype(jnp.bfloat16)
    return act, (grad_act * (cumul + hidden_pre * density)).astype(jnp.bfloat16)


def swap(value, axis, size, mask):
    return lax.ppermute(value, axis, [(i, i ^ mask) for i in range(size)])


def transposed(value, rows, cols):
    per = cols // rows
    pairs = [
        (r * cols + c, (c // per) * cols + r * per + c % per) for r in range(rows) for c in range(cols)
    ]
    return lax.ppermute(value, ("row", "col"), pairs)


def streamed(sources, slots, sems, count, use):
    depth = slots[0].shape[0]

    def copies(j):
        return [
            pltpu.make_async_copy(source(j), slot.at[j % depth], sems.at[i, j % depth])
            for i, (source, slot) in enumerate(zip(sources, slots))
        ]

    for j in range(min(depth - 1, count)):
        for copy in copies(j):
            copy.start()
    for j in range(count):
        if j + depth - 1 < count:
            for copy in copies(j + depth - 1):
                copy.start()
        for copy in copies(j):
            copy.wait()
        use(j, j % depth)


def store_kernel(firsts, hidden, at_ref, *refs):
    arrays, sems = refs[-3:-1], refs[-1]
    copies = []
    for i, first in enumerate(firsts):
        for j, block in enumerate(refs[2 * i : 2 * i + 2]):
            n, f = block.shape[1:]
            side = at_ref[0] if j == 0 else 1 - at_ref[0]
            for k in range(2):
                if hidden:
                    rows = arrays[k].at[pl.ds(first + j * n, n)]
                else:
                    rows = arrays[k].at[pl.ds(first, n), pl.ds(pl.multiple_of(side * f, f), f)]
                copies.append((block.at[k], rows))
    copies = [pltpu.make_async_copy(*pair, sems.at[i]) for i, pair in enumerate(copies)]
    for copy in copies:
        copy.start()
    for copy in copies:
        copy.wait()


def stored(at, firsts, pieces, hidden, total):
    inputs = [piece for part in pieces for piece in part]
    width = inputs[0].shape[2] * (1 if hidden else 2)
    return pl.pallas_call(
        functools.partial(store_kernel, firsts, hidden),
        out_shape=[jax.ShapeDtypeStruct((total, width), jnp.bfloat16)] * 2,
        in_specs=[SMEM] + [pl.BlockSpec(memory_space=pl.ANY)] * len(inputs),
        out_specs=[VMEM] * 2,
        scratch_shapes=[pltpu.SemaphoreType.DMA((2 * len(inputs),))],
        compiler_params=pltpu.CompilerParams(vmem_limit_bytes=LIMIT),
        cost_estimate=pl.CostEstimate(flops=COST, bytes_accessed=0, transcendentals=0),
    )(at, *inputs)


def in_kernel(stream, at_ref, mine, other, weight_in, weight_out, *refs):
    away, keep, panel, *streaming = refs
    half, f = keep.shape[1], panel.shape[2] // 2
    side = at_ref[0]
    panel[:, :, pl.ds(pl.multiple_of(side * f, f), f)] = mine[...]
    panel[:, :, pl.ds(pl.multiple_of((1 - side) * f, f), f)] = other[...]
    tile = 512

    def use(j, in_tile, out_tile):
        cols = slice(j * tile, (j + 1) * tile)
        hidden = contract(panel[0], in_tile, 1, 0)
        keep[0, :, cols] = hidden[:half]
        away[0, :, cols] = hidden[half:].astype(away.dtype)
        grad = contract(panel[1], out_tile, 1, 1)
        keep[1, :, cols] = grad[:half]
        away[1, :, cols] = grad[half:].astype(away.dtype)

    count = weight_in.shape[1] // tile
    if stream:
        in_slots, out_slots, sems = streaming
        streamed(
            [lambda j: weight_in.at[:, pl.ds(j * tile, tile)], lambda j: weight_out.at[pl.ds(j * tile, tile)]],
            [in_slots, out_slots],
            sems,
            count,
            lambda j, slot: use(j, in_slots[slot], out_slots[slot]),
        )
    else:
        for j in range(count):
            cols = slice(j * tile, (j + 1) * tile)
            use(j, weight_in[:, cols], weight_out[cols])


def out_kernel(at_ref, own, got, weight_in, weight_out, away, keep, full):
    half, f = own.shape[1], keep.shape[2]
    full[:, :half] = own[...]
    full[:, half:] = got[...]
    tile = 256
    for out, side in ((away, 1 - at_ref[0]), (keep, at_ref[0])):
        for j in range(f // tile):
            cols = slice(j * tile, (j + 1) * tile)
            at = pl.ds(pl.multiple_of(side * f + j * tile, tile), tile)
            out[0, :, cols] = contract(full[0], weight_out[:, at], 1, 0).astype(out.dtype)
            out[1, :, cols] = contract(full[1], weight_in[at, :], 1, 1).astype(out.dtype)


def terms_call(kernel, at, blocks, weights, shape, panel_shape, slots=()):
    return pl.pallas_call(
        kernel,
        out_shape=[jax.ShapeDtypeStruct(shape, jnp.bfloat16), jax.ShapeDtypeStruct(shape, jnp.float32)],
        in_specs=[SMEM] + [VMEM] * len(blocks) + [HBM if slots else VMEM] * len(weights),
        out_specs=[VMEM, VMEM],
        scratch_shapes=[
            pltpu.VMEM(panel_shape, jnp.bfloat16),
            *[pltpu.VMEM(slot, jnp.bfloat16) for slot in slots],
            *[pltpu.SemaphoreType.DMA((2, slot[0])) for slot in slots[:1]],
        ],
        compiler_params=pltpu.CompilerParams(vmem_limit_bytes=STREAM_LIMIT if slots else LIMIT),
        cost_estimate=pl.CostEstimate(flops=COST, bytes_accessed=0, transcendentals=0),
    )(at, *blocks, *weights)


def in_terms(at, blocks, weights, stream):
    width, ff = weights[0].shape
    n = blocks[0].shape[1]
    return terms_call(
        functools.partial(in_kernel, stream),
        at,
        blocks,
        weights,
        (2, n // 2, ff),
        (2, n, width),
        [(3, width, 512), (3, 512, width)] if stream else (),
    )


def out_terms(at, own, got, weights):
    width, ff = weights[0].shape
    n = 2 * own.shape[1]
    return terms_call(out_kernel, at, (own, got), weights, (2, n, width // 2), (2, n, ff))


class Clock:
    def __init__(self):
        self.last = None

    def start(self, value):
        if self.last is None:
            return value
        return lax.optimization_barrier((value, self.last))[0]

    def end(self, value):
        self.last = value
        return value


class Grid:
    def __init__(self, rows, cols, clock):
        self.rows, self.cols, self.clock = rows, cols, clock
        self.core = lax.axis_index("row") % 2
        self.at = jnp.reshape(lax.axis_index("col") % 2, (1,)).astype(jnp.int32)

    def gather(self, block):
        clock = self.clock
        block = transposed(clock.end(clock.start(block)), self.rows, self.cols)
        yield
        block = clock.end(clock.start(block))
        far = swap(block, "col", self.cols, 4)
        yield
        near = clock.end(jnp.concatenate([block, clock.start(far)], axis=1))
        far = swap(near, "col", self.cols, 2)
        yield
        far = clock.start(far)
        mine = jnp.where(
            self.core == 0,
            jnp.concatenate([near, far], axis=1),
            jnp.concatenate([far, near], axis=1),
        )
        mine = clock.end(mine)
        other = swap(mine, "col", self.cols, 1)
        yield
        return mine, clock.start(other)

    def scatter(self, away, keep):
        clock, n = self.clock, keep.shape[1] // 4
        clock.end(away)
        got = swap(away, "col", self.cols, 1)
        yield
        total = keep + clock.start(got)
        away = lax.dynamic_slice_in_dim(total, (1 - self.core) * 2 * n, 2 * n, axis=1)
        away = clock.end(away.astype(jnp.bfloat16))
        keep = lax.dynamic_slice_in_dim(total, self.core * 2 * n, 2 * n, axis=1)
        got = swap(away, "col", self.cols, 2)
        yield
        total = keep + clock.start(got)
        away = clock.end(total[:, n:].astype(jnp.bfloat16))
        got = swap(away, "col", self.cols, 4)
        yield
        out = clock.end((total[:, :n] + clock.start(got)).astype(jnp.bfloat16))
        out = transposed(out, self.rows, self.cols)
        yield
        return clock.end(clock.start(out))


def part_steps(grid, block, weights, stream, made):
    clock, rows = grid.clock, grid.rows
    made["tokens"] = blocks = yield from grid.gather(block)
    away, keep = in_terms(grid.at, blocks, weights, stream)
    got = swap(clock.end(away), "row", rows, 1)
    yield
    sums = keep + clock.start(got)
    got = swap(clock.end(sums.astype(jnp.bfloat16)), "row", rows, 2)
    yield
    act, grad_pre = activations(sums + clock.start(got))
    own = clock.end(jnp.stack([act, grad_pre]))
    got = swap(own, "row", rows, 1)
    yield
    got = clock.start(got)
    made["hidden"] = own, got
    made["out"] = yield from grid.scatter(*out_terms(grid.at, own, got, weights))


def body(rows, cols, tokens, weight_in, weight_out, out_grad):
    clock = Clock()
    grid = Grid(rows, cols, clock)
    both = jnp.stack([tokens, out_grad])
    count = tokens.shape[0]
    size = [count * share // sum(SHARES) for share in SHARES]
    start = [sum(size[:part]) for part in range(len(size))]
    made = [{} for _ in size]
    parts = [
        part_steps(grid, both[:, at : at + n], (weight_in, weight_out), not at, out)
        for at, n, out in zip(start, size, made)
    ]
    arrays, grads = [], []
    for part in ORDER:
        if part == -2:
            pieces = [out["hidden" if arrays else "tokens"] for out in made]
            pieces[0] = (clock.start(pieces[0][0]), pieces[0][1])
            arrays += stored(grid.at, [rows * at for at in start], pieces, bool(arrays), rows * count)
            clock.end(arrays[-1])
        elif part == -1:
            panel, full = arrays[len(grads)], clock.start(arrays[3 - len(grads)])
            grad = contract(full, panel, 0, 0) if grads else contract(panel, full, 0, 0)
            grads.append(clock.end(grad.astype(jnp.bfloat16)))
        else:
            next(parts[part], None)
    out = jnp.concatenate([m["out"] for m in made], axis=1)
    return out[0], out[1], grads[0], grads[1]


def plain_body(rows, cols, tokens, weight_in, weight_out, out_grad):
    per = cols // rows
    both = jnp.stack([tokens, out_grad])
    two, n, f = both.shape
    panel = lax.all_gather(transposed(both, rows, cols), "col", axis=0)
    panel = panel.reshape(rows, per, two, n, f).transpose(2, 0, 3, 1, 4).reshape(two, rows * n, per * f)
    terms = jnp.stack([contract(panel[0], weight_in, 1, 0), contract(panel[1], weight_out, 1, 1)])
    act, grad_pre = activations(lax.psum_scatter(terms, "row", scatter_dimension=1, tiled=True))
    full = lax.all_gather(jnp.stack([act, grad_pre]), "row", axis=1, tiled=True)
    terms = jnp.stack([contract(full[0], weight_out, 1, 0), contract(full[1], weight_in, 1, 1)])
    terms = terms.reshape(two, rows, n, per, f).transpose(1, 3, 0, 2, 4).reshape(cols, two, n, f)
    out = lax.psum_scatter(terms, "col", scatter_dimension=0).astype(jnp.bfloat16)
    out = transposed(out, rows, cols)
    grad_in = contract(panel[0], full[1], 0, 0).astype(jnp.bfloat16)
    grad_out = contract(full[0], panel[1], 0, 0).astype(jnp.bfloat16)
    return out[0], out[1], grad_in, grad_out


def solution(mesh):
    shape = (mesh.shape["row"], mesh.shape["col"])
    return jax.shard_map(
        functools.partial(body if shape == (4, 8) else plain_body, *shape),
        mesh=mesh,
        in_specs=(P("row", "col"), P("row", "col"), P("col", "row"), P("row", "col")),
        out_specs=(P("row", "col"), P("row", "col"), P("row", "col"), P("col", "row")),
        check_vma=False,
    )
```
